128 devices in a mesh: rep: 16 (over z_lo, y, core), tp: 8 (over z_hi, x).
Axes of the slice: x: 4, y: 4, z: 4 (z_hi: 2, z_lo: 2; z = z_hi * 2 + z_lo), core: 2. Of those that a mesh axis runs over, the one named last changes fastest.
Arguments:
- normed: bfloat16 [64, 128, 4096], P('rep', None, 'tp'), may hold values from -6 to 6
- documents: int32 [64, 128], P('rep'), may hold values from 0 to 15, never falling along the last dimension, each value on 1 to 64 neighbouring positions
- cotangent: bfloat16 [64, 128, 4096], P('rep'), may hold values from -6 to 6
- w_query: bfloat16 [16, 4096, 4096], P('rep', None, 'tp'), may hold values from -6 to 6
- w_key: bfloat16 [16, 4096, 1024], P('rep', None, 'tp'), may hold values from -6 to 6
- w_value: bfloat16 [16, 4096, 1024], P('rep', None, 'tp'), may hold values from -6 to 6
- w_out: bfloat16 [16, 4096, 4096], P('rep', 'tp'), may hold values from -6 to 6
- step_index: int32 [1], replicated, may hold values from 0 to 63
Outputs:
- layer_out: bfloat16 [64, 128, 4096], P('rep', None, 'tp')
- new_query: bfloat16 [16, 4096, 4096], P('rep', None, 'tp')
- new_key: bfloat16 [16, 4096, 1024], P('rep', None, 'tp')
- new_value: bfloat16 [16, 4096, 1024], P('rep', None, 'tp')
- new_out: bfloat16 [16, 4096, 4096], P('rep', 'tp')
The draws below stay inside these ranges and needn't reach their ends.
All inputs are finite; a program needn't handle non-finite values.
Results may differ from the reference program's by a relative error of at most 0.017.
Values may be sent and summed in bfloat16 or wider, within the bound.
A program may use at most 192 MiB of HBM per device.

```python
import math
import jax
import jax.numpy as jnp
import numpy as np
from jax import lax

D = 4096
HEADS = 32
KV_HEADS = 8
HEAD = 128
SEQ = 128
SEQS = 4
ROWS = 64
N_REP = 16


def draw_normed(key, part):
    key = jax.random.fold_in(key, 11)
    base = jnp.clip(jax.random.normal(key, (ROWS, SEQ, D), jnp.float32), -6.0, 6.0)
    return base.astype(jnp.bfloat16)


def steps_of(rng, extent, cuts, low, top_value):
    factor_of, own = 1.0, jax.random.fold_in(rng, 6)
    for dim, shards_of in cuts:
        draws = jnp.exp(jax.random.uniform(jax.random.fold_in(own, dim), (shards_of,), jnp.float32, low / len(cuts), top_value / len(cuts)))
        factor_of = factor_of * jnp.repeat(draws, extent[dim] // shards_of).reshape([-1 if axis == dim else 1 for axis in range(len(extent))])
    return factor_of


def split_up(number_of, total, reach, slope):
    weights = [(1 << 20) // math.isqrt(grade ** slope) + 1 for grade in range(2, number_of + 1)]
    surplus, given = total - reach - (number_of - 1), [1] * (number_of - 1)
    while surplus > 0:
        candidates = [i for i in range(number_of - 1) if given[i] < reach]
        pool, remaining = sum([weights[i] for i in candidates]), surplus
        for i in candidates:
            extra = min(reach - given[i], max(1, remaining * weights[i] // pool), surplus)
            given[i] = given[i] + extra
            surplus = surplus - extra
    return np.array([reach] + given)


def uneven_parts(rng, count, total, reach, skew):
    if count == 2:
        one = jax.random.randint(rng, (), max(1, total - reach), min(reach, total - 1) + 1)
        return jnp.stack([one, total - one])
    lengths = jnp.asarray(split_up(count, total, reach, skew), jnp.int32)
    pairs = (count - 1) // 2
    source_of, receiver = lengths[1:1 + 2 * pairs:2], lengths[2:2 + 2 * pairs:2]
    margin = jnp.minimum(source_of - 1, reach - receiver)
    shifted = jax.random.randint(jax.random.fold_in(rng, 1), (pairs,), 0, 1 << 20) % (margin + 1)
    lengths = lengths.at[1:1 + 2 * pairs:2].set(source_of - shifted).at[2:2 + 2 * pairs:2].set(receiver + shifted)
    return lengths[jax.random.permutation(jax.random.fold_in(rng, 2), count)]


def bell_draw(key, extent, spread, reach, cuts=(), kind=jnp.bfloat16):
    values = jax.random.normal(key, extent, jnp.float32) * spread
    if len(cuts) > 0:
        values = steps_of(key, extent, cuts, -0.22, 0.18) * values
    return jnp.clip(values, min=-reach, max=reach).astype(kind)


def setup_inputs(seed: int = 0) -> dict:
    streams_of = jax.random.split(jax.random.key(seed), 9)
    return {
        "normed": draw_normed(jax.random.fold_in(streams_of[8], 71), 0),
        "documents": jax.vmap(lambda own: jnp.searchsorted(jnp.cumsum(uneven_parts(own, SEQ // 8, SEQ, SEQ // 2, 2)), jnp.arange(SEQ), side="right"))(jax.random.split(streams_of[1], ROWS)).reshape((ROWS, SEQ)).astype(jnp.int32),
        "cotangent": bell_draw(streams_of[2], (ROWS, SEQ, D), 1.0, 6.0, ((0, 16),)),
        "w_query": bell_draw(streams_of[3], (N_REP, D, HEADS * HEAD), 1.0, 6.0, ((0, 16), (2, 8))),
        "w_key": bell_draw(streams_of[4], (N_REP, D, KV_HEADS * HEAD), 1.0, 6.0, ((0, 16), (2, 8))),
        "w_value": bell_draw(streams_of[5], (N_REP, D, KV_HEADS * HEAD), 1.0, 6.0, ((0, 16), (2, 8))),
        "w_out": bell_draw(streams_of[6], (N_REP, HEADS * HEAD, D), 1.0, 6.0, ((0, 16), (1, 8))),
        "step_index": jax.random.randint(streams_of[7], (1,), 0, 64).astype(jnp.int32),
    }


def rotate(values, positions):
    half_dim = values.shape[-1] // 2
    frequency = 500000.0 ** (-jnp.arange(half_dim, dtype=jnp.float32) / half_dim)
    angles = positions[:, None].astype(jnp.float32) * frequency[None, :]
    cosine = jnp.cos(angles)[None, :, None, :]
    sine_part = jnp.sin(angles)[None, :, None, :]
    front_part = values[..., :half_dim]
    second = values[..., half_dim:]
    return jnp.concatenate([front_part * cosine - second * sine_part, second * cosine + front_part * sine_part], axis=-1)

def attend(params, normed, documents):
    w_query, w_key, w_value, w_out = params
    batch, length, width = normed.shape
    flat = normed.reshape(batch * length, width)
    scale_in = 1.0 / math.sqrt(width)
    q_heads = w_query.shape[1] // HEAD
    kv_heads = w_key.shape[1] // HEAD
    positions = jnp.arange(length)
    queries = jnp.dot(flat, w_query, preferred_element_type=jnp.float32) * scale_in
    queries = rotate(queries.reshape(batch, length, q_heads, HEAD), positions).astype(jnp.bfloat16)
    keys_all = jnp.dot(flat, w_key, preferred_element_type=jnp.float32) * scale_in
    keys_all = rotate(keys_all.reshape(batch, length, kv_heads, HEAD), positions).astype(jnp.bfloat16)
    values_all = (jnp.dot(flat, w_value, preferred_element_type=jnp.float32) * scale_in).astype(jnp.bfloat16)
    values_all = values_all.reshape(batch, length, kv_heads, HEAD)
    group_size = q_heads // kv_heads
    queries = queries.reshape(batch, length, kv_heads, group_size, HEAD)
    scores = jnp.einsum('bqkgd,bskd->bkgqs', queries.astype(jnp.float32), keys_all.astype(jnp.float32)) / math.sqrt(HEAD)
    causal = positions[None, :] <= positions[:, None]
    same_doc = documents[:, :, None] == documents[:, None, :]
    allowed = jnp.logical_and(causal[None], same_doc)
    scores = jnp.where(allowed[:, None, None], scores, -1000000000.0)
    probs = jax.nn.softmax(scores, axis=-1).astype(jnp.bfloat16)
    mixed = jnp.einsum('bkgqs,bskd->bqkgd', probs.astype(jnp.float32), values_all.astype(jnp.float32)).astype(jnp.bfloat16)
    mixed = mixed.reshape(batch * length, q_heads * HEAD)
    output = jnp.dot(mixed, w_out, preferred_element_type=jnp.float32) * scale_in
    return output.reshape(batch, length, width)

def reference(normed, documents, cotangent, w_query, w_key, w_value, w_out, step_index):
    replicas = w_query.shape[0]
    normed_r = normed.reshape(replicas, SEQS, SEQ, D)
    docs_r = documents.reshape(replicas, SEQS, SEQ)
    cot_r = cotangent.reshape(replicas, SEQS, SEQ, D)

    def replica(inputs):
        inputs_x, inputs_doc, inputs_cot, query_w, key_w, value_w, out_w = inputs

        def local(params):
            return attend(params, inputs_x, inputs_doc)
        result, pull = jax.vjp(local, (query_w, key_w, value_w, out_w))
        grads = pull(inputs_cot.astype(jnp.float32))[0]
        grads = tuple((grad.astype(jnp.bfloat16) for grad in grads))
        return (result.astype(jnp.bfloat16), grads)
    outputs, grads = lax.map(replica, (normed_r, docs_r, cot_r, w_query, w_key, w_value, w_out))
    levels = replicas.bit_length() - 1
    distance = (2 ** (step_index[0] % levels)).astype(jnp.int32)
    rate_now = 3.0 * 32.0 / (32.0 + step_index[0].astype(jnp.float32))

    def average(weight, gradient):
        updated = (weight.astype(jnp.float32) - rate_now * gradient.astype(jnp.float32)).astype(jnp.bfloat16)
        peer_u = jnp.roll(updated, distance, axis=0)
        return (0.5 * (updated.astype(jnp.float32) + peer_u.astype(jnp.float32))).astype(jnp.bfloat16)
    new_query = average(w_query, grads[0])
    new_key = average(w_key, grads[1])
    new_value = average(w_value, grads[2])
    new_out = average(w_out, grads[3])
    return (outputs.reshape(replicas * SEQS, SEQ, D), new_query, new_key, new_value, new_out)
```

```python
import functools
import math

import jax
import jax.numpy as jnp
import numpy as np
from jax import lax
from jax.experimental import pallas as pl
from jax.experimental.pallas import tpu as pltpu
from jax.sharding import PartitionSpec as P

HEAD = 128
SEQS = 4
SEQ = 128
TOKENS = SEQS * SEQ
X_CHIPS = 4
Y_CHIPS = 4
TP = 8
D = 4096
SLAB = D // TP
Q_HEADS = 4
Q_COLS = Q_HEADS * HEAD
QKV = Q_COLS + 2 * HEAD
SCALE = 1.0 / math.sqrt(D)
SCORE_SCALE = 1.0 / math.sqrt(HEAD)
MESH = pl.DeviceIdType.MESH
F32 = jnp.float32
BF16 = jnp.bfloat16


def rotation_tables():
    half = HEAD // 2
    frequency = (500000.0 ** (-np.arange(half, dtype=np.float64) / half)).astype(np.float32)
    angles = np.arange(SEQ, dtype=np.float32)[:, None] * frequency[None, :]
    cosine, sine = np.cos(angles), np.sin(angles)
    return (
        np.concatenate([cosine, cosine], axis=1).astype(np.float32),
        np.concatenate([-sine, sine], axis=1).astype(np.float32),
    )


def dot(a, b, contract):
    return lax.dot_general(
        a, b, (((contract[0],), (contract[1],)), ((), ())), preferred_element_type=F32
    )


def turned(values, cosine, sine):
    return values * cosine + pltpu.roll(values, HEAD // 2, 1) * sine


def front_kernel(
    x_in, cot_in, wq_in, wk_in, wv_in, wo_in, docs, cos_ref, sin_ref,
    x_out, mixed_out, dqkv_out,
    x_all, cot, w_qkv, w_o, acc, d_mixed,
    send_sems, recv_sems, load_sems, store_sems,
):
    me = lax.axis_index("tp")
    x, z = me % X_CHIPS, me // X_CHIPS
    right = z * X_CHIPS + (x + 1) % X_CHIPS
    left = z * X_CHIPS + (x + 3) % X_CHIPS
    far = z * X_CHIPS + (x + 2) % X_CHIPS
    across = (1 - z) * X_CHIPS + x
    across_right = (1 - z) * X_CHIPS + (x + 1) % X_CHIPS
    across_left = (1 - z) * X_CHIPS + (x + 3) % X_CHIPS
    across_far = (1 - z) * X_CHIPS + (x + 2) % X_CHIPS

    barrier = pltpu.get_barrier_semaphore()
    for peer in (left, right, across):
        pl.semaphore_signal(barrier, inc=1, device_id={"tp": peer}, device_id_type=MESH)
    loads = [
        pltpu.make_async_copy(cot_in, cot, load_sems.at[0]),
        pltpu.make_async_copy(wo_in, w_o, load_sems.at[1]),
        pltpu.make_async_copy(x_in, x_all.at[me], load_sems.at[2]),
        pltpu.make_async_copy(wq_in, w_qkv.at[:, pl.ds(0, Q_COLS)], load_sems.at[3]),
        pltpu.make_async_copy(wk_in, w_qkv.at[:, pl.ds(Q_COLS, HEAD)], load_sems.at[4]),
        pltpu.make_async_copy(wv_in, w_qkv.at[:, pl.ds(Q_COLS + HEAD, HEAD)], load_sems.at[5]),
    ]
    pl.semaphore_wait(barrier, 3)

    def remote(src, dst, peer, index):
        return pltpu.make_async_remote_copy(
            src_ref=src, dst_ref=dst, send_sem=send_sems.at[index], recv_sem=recv_sems.at[index],
            device_id={"tp": peer}, device_id_type=MESH,
        )

    upper, lower = pl.ds(0, TOKENS // 2), pl.ds(TOKENS // 2, TOKENS // 2)
    own = x_all.at[me]
    to_right = remote(x_in, own, right, 0)
    to_left = remote(x_in, own, left, 1)
    to_across = remote(x_in, own, across, 2)
    part = x_all.at[left, upper]
    far_right = remote(part, part, right, 3)
    part = x_all.at[right, lower]
    far_left = remote(part, part, left, 4)
    part = x_all.at[across]
    across_to_right = remote(part, part, right, 5)
    across_to_left = remote(part, part, left, 6)
    part = x_all.at[far]
    far_to_across = remote(part, part, across, 7)

    to_right.start()
    to_left.start()
    to_across.start()
    for load in loads:
        load.start()
    for load in loads[:2]:
        load.wait()

    acc[:, :Q_COLS] = jnp.zeros((TOKENS, Q_COLS), F32)

    @pl.loop(0, TP)
    def _(step):
        columns = pl.ds(pl.multiple_of(step * SLAB, SLAB), SLAB)
        acc[:, :Q_COLS] += dot(cot[:, columns], w_o[:, columns], (1, 1))

    d_mixed[...] = (acc[:, :Q_COLS] * SCALE).astype(BF16)

    for load in loads[2:]:
        load.wait()
    stores = []

    def project(block, index):
        store = pltpu.make_async_copy(x_all.at[block], x_out.at[block], store_sems.at[index])
        store.start()
        stores.append(store)
        rows = pl.ds(pl.multiple_of(block * SLAB, SLAB), SLAB)

        @pl.loop(0, QKV // 256)
        def _(step):
            columns = pl.ds(pl.multiple_of(step * 256, 256), 256)
            term = dot(x_all[block], w_qkv[rows, columns], (1, 0))
            if index == 0:
                acc[:, columns] = term
            else:
                acc[:, columns] += term

    project(me, 0)
    to_right.wait_recv()
    far_right.start()
    to_left.wait_recv()
    far_left.start()
    project(left, 1)
    to_across.wait_recv()
    across_to_right.start()
    across_to_left.start()
    project(right, 2)
    far_right.wait_recv()
    far_left.wait_recv()
    far_to_across.start()
    project(across, 3)
    project(far, 4)
    across_to_right.wait_recv()
    project(across_left, 5)
    across_to_left.wait_recv()
    project(across_right, 6)
    far_to_across.wait_recv()
    project(across_far, 7)

    cosine, sine = cos_ref[...], sin_ref[...]
    later = lax.broadcasted_iota(jnp.int32, (SEQ, SEQ), 0)
    earlier = lax.broadcasted_iota(jnp.int32, (SEQ, SEQ), 1)
    causal = earlier <= later
    heads = range(Q_HEADS)

    for sequence in range(SEQS):
        rows = slice(sequence * SEQ, (sequence + 1) * SEQ)

        def stacked(pieces):
            return jnp.concatenate(pieces, axis=0)

        queries = stacked(
            [
                turned(acc[rows, h * HEAD : (h + 1) * HEAD] * SCALE, cosine, sine).astype(BF16)
                for h in heads
            ]
        )
        keys = turned(acc[rows, Q_COLS : Q_COLS + HEAD] * SCALE, cosine, sine).astype(BF16)
        values = (acc[rows, Q_COLS + HEAD :] * SCALE).astype(BF16)
        number = jnp.broadcast_to(docs[sequence : sequence + 1, :].astype(F32), (SEQ, SEQ))
        allowed = jnp.logical_and(causal, number == number.T)
        scores = dot(queries, keys, (1, 1)) * SCORE_SCALE
        scores = stacked(
            [jnp.where(allowed, scores[h * SEQ : (h + 1) * SEQ], -1e9) for h in heads]
        )
        exps = jnp.exp(scores - jnp.max(scores, axis=1, keepdims=True))
        probs = exps / jnp.sum(exps, axis=1, keepdims=True)
        rounded = probs.astype(BF16)
        mixed = dot(rounded, values, (1, 0)).astype(BF16)
        d_heads = stacked([d_mixed[rows, h * HEAD : (h + 1) * HEAD] for h in heads])
        d_probs = dot(d_heads, values, (1, 1)).astype(BF16).astype(F32)
        d_values = dot(rounded, d_heads, (0, 0)).astype(BF16)
        d_scores = probs * (d_probs - jnp.sum(d_probs * probs, axis=1, keepdims=True))
        d_scores = (d_scores * SCORE_SCALE).astype(BF16)
        d_queries = dot(d_scores, keys, (1, 0)).astype(BF16).astype(F32)
        d_keys = dot(d_scores, queries, (0, 0)).astype(BF16).astype(F32)
        for h in heads:
            columns = slice(h * HEAD, (h + 1) * HEAD)
            stack = slice(h * SEQ, (h + 1) * SEQ)
            mixed_out[rows, columns] = mixed[stack]
            dqkv_out[rows, columns] = (turned(d_queries[stack], cosine, -sine) * SCALE).astype(BF16)
        dqkv_out[rows, Q_COLS : Q_COLS + HEAD] = (turned(d_keys, cosine, -sine) * SCALE).astype(BF16)
        dqkv_out[rows, Q_COLS + HEAD :] = (d_values.astype(F32) * SCALE).astype(BF16)

    for copy in (
        to_right, to_left, to_across, far_right, far_left,
        across_to_right, across_to_left, far_to_across,
    ):
        copy.wait_send()
    for store in stores:
        store.wait()


def front(normed, cotangent, w_query, w_key, w_value, w_out, documents):
    cosine, sine = rotation_tables()
    hbm = pl.BlockSpec(memory_space=pl.ANY)
    vmem = pl.BlockSpec(memory_space=pltpu.VMEM)
    return pl.pallas_call(
        front_kernel,
        name="gather_and_attend",
        out_shape=(
            jax.ShapeDtypeStruct((TP, TOKENS, SLAB), BF16),
            jax.ShapeDtypeStruct((TOKENS, Q_COLS), BF16),
            jax.ShapeDtypeStruct((TOKENS, QKV), BF16),
        ),
        in_specs=[hbm] * 6 + [vmem] * 3,
        out_specs=(hbm, vmem, vmem),
        scratch_shapes=[
            pltpu.VMEM((TP, TOKENS, SLAB), BF16),
            pltpu.VMEM((TOKENS, D), BF16),
            pltpu.VMEM((D, QKV), BF16),
            pltpu.VMEM((Q_COLS, D), BF16),
            pltpu.VMEM((TOKENS, QKV), F32),
            pltpu.VMEM((TOKENS, Q_COLS), BF16),
            pltpu.SemaphoreType.DMA((8,)),
            pltpu.SemaphoreType.DMA((8,)),
            pltpu.SemaphoreType.DMA((6,)),
            pltpu.SemaphoreType.DMA((8,)),
        ],
        compiler_params=pltpu.CompilerParams(
            collective_id=0, has_side_effects=True, vmem_limit_bytes=48 * 1024 * 1024
        ),
        cost_estimate=pl.CostEstimate(
            flops=6_000_000_000, bytes_accessed=20_000_000, transcendentals=300_000
        ),
    )(normed, cotangent, w_query, w_key, w_value, w_out, documents, cosine, sine)


def moved(weight, gradient, rate):
    gradient = gradient.astype(BF16).astype(F32)
    return (weight.astype(F32) - rate * gradient).astype(BF16)


def out_update_kernel(rate, mixed, cot, w_o, updated):
    gradient = dot(mixed[...], cot[...], (0, 0)) * SCALE
    updated[...] = moved(w_o[...], gradient, rate[0])


def out_update(rate, mixed, cotangent, w_out):
    width = 1024
    wide = pl.BlockSpec((TOKENS, width), lambda i: (0, i))
    return pl.pallas_call(
        out_update_kernel,
        name="update_out",
        grid=(D // width,),
        out_shape=jax.ShapeDtypeStruct((Q_COLS, D), BF16),
        in_specs=[
            pl.BlockSpec(memory_space=pltpu.SMEM),
            pl.BlockSpec((TOKENS, Q_COLS), lambda i: (0, 0)),
            wide,
            wide,
        ],
        out_specs=wide,
        compiler_params=pltpu.CompilerParams(vmem_limit_bytes=32 * 1024 * 1024),
        cost_estimate=pl.CostEstimate(
            flops=2 * TOKENS * Q_COLS * D, bytes_accessed=13_000_000, transcendentals=0
        ),
    )(rate, mixed, cotangent, w_out)


def in_update_kernel(rate, x_all, dqkv, w_q, w_k, w_v, new_q, new_k, new_v):
    gradient = dot(x_all[0], dqkv[...], (0, 0))
    new_q[...] = moved(w_q[...], gradient[:, :Q_COLS], rate[0])
    new_k[...] = moved(w_k[...], gradient[:, Q_COLS : Q_COLS + HEAD], rate[0])
    new_v[...] = moved(w_v[...], gradient[:, Q_COLS + HEAD :], rate[0])


def in_update(rate, x_all, dqkv, w_query, w_key, w_value):
    wide = pl.BlockSpec((SLAB, Q_COLS), lambda i: (i, 0))
    slim = pl.BlockSpec((SLAB, HEAD), lambda i: (i, 0))
    return pl.pallas_call(
        in_update_kernel,
        name="update_qkv",
        grid=(TP,),
        out_shape=(
            jax.ShapeDtypeStruct((D, Q_COLS), BF16),
            jax.ShapeDtypeStruct((D, HEAD), BF16),
            jax.ShapeDtypeStruct((D, HEAD), BF16),
        ),
        in_specs=[
            pl.BlockSpec(memory_space=pltpu.SMEM),
            pl.BlockSpec((1, TOKENS, SLAB), lambda i: (i, 0, 0)),
            pl.BlockSpec((TOKENS, QKV), lambda i: (0, 0)),
            wide,
            slim,
            slim,
        ],
        out_specs=(wide, slim, slim),
        compiler_params=pltpu.CompilerParams(vmem_limit_bytes=32 * 1024 * 1024),
        cost_estimate=pl.CostEstimate(
            flops=2 * TOKENS * QKV * D, bytes_accessed=18_000_000, transcendentals=0
        ),
    )(rate, x_all, dqkv, w_query, w_key, w_value)


def passed_along(value, distance):
    count = lax.axis_size("rep")
    pairs = [(source, (source + distance) % count) for source in range(count)]
    return lax.ppermute(value, "rep", pairs)


def average(own, peer):
    return (0.5 * (own.astype(F32) + peer.astype(F32))).astype(BF16)


def finish(distance, rate, x_all, mixed, dqkv, cotangent, w_query, w_key, w_value, w_out):
    new_o = out_update(rate, mixed, cotangent, w_out)
    peer_o = passed_along(new_o, distance)
    updated = in_update(rate, x_all, dqkv, w_query, w_key, w_value)
    peers = [passed_along(u, distance) for u in updated]
    partial = (jnp.dot(mixed, w_out, preferred_element_type=F32) * SCALE).astype(BF16)
    layer_out = lax.psum_scatter(
        partial.reshape(SEQS, SEQ, D), "tp", scatter_dimension=2, tiled=True
    )
    new = [average(u, p)[None] for u, p in zip((*updated, new_o), (*peers, peer_o))]
    return (layer_out, *new)


def per_device(normed, documents, cotangent, w_query, w_key, w_value, w_out, step_index):
    levels = lax.axis_size("rep").bit_length() - 1
    level = step_index[0] % levels
    rate = 3.0 * 32.0 / (32.0 + step_index.astype(F32))
    flat = cotangent.reshape(TOKENS, D)
    weights = (w_query[0], w_key[0], w_value[0], w_out[0])
    x_all, mixed, dqkv = front(normed.reshape(TOKENS, SLAB), flat, *weights, documents)
    return lax.switch(
        level,
        [functools.partial(finish, 2**exponent) for exponent in range(levels)],
        rate, x_all, mixed, dqkv, flat, *weights,
    )


def solution(mesh):
    in_specs = (
        P("rep", None, "tp"),
        P("rep", None),
        P("rep", None, None),
        P("rep", None, "tp"),
        P("rep", None, "tp"),
        P("rep", None, "tp"),
        P("rep", "tp", None),
        P(),
    )
    out_specs = (
        P("rep", None, "tp"),
        P("rep", None, "tp"),
        P("rep", None, "tp"),
        P("rep", None, "tp"),
        P("rep", "tp", None),
    )
    return jax.shard_map(
        per_device, mesh=mesh, in_specs=in_specs, out_specs=out_specs, check_vma=False
    )
```

```python
import functools
import math

import jax
import jax.numpy as jnp
import numpy as np
from jax import lax
from jax.experimental import pallas as pl
from jax.experimental.pallas import tpu as pltpu
from jax.sharding import PartitionSpec as P

HEAD = 128
SEQS = 4
SEQ = 128
TOKENS = SEQS * SEQ
X_CHIPS = 4
Y_CHIPS = 4
TP = 8
D = 4096
SLAB = D // TP
Q_HEADS = 4
Q_COLS = Q_HEADS * HEAD
QKV = Q_COLS + 2 * HEAD
DIRECT_ROWS = 192
AROUND_ROWS = Q_COLS - DIRECT_ROWS
O_STEPS = 4
O_COLS = D // O_STEPS
WINDOW = 6
SCALE = 1.0 / math.sqrt(D)
SCORE_SCALE = 1.0 / math.sqrt(HEAD)
MESH = pl.DeviceIdType.MESH
F32 = jnp.float32
BF16 = jnp.bfloat16


def rotation_tables():
    half = HEAD // 2
    frequency = (500000.0 ** (-np.arange(half, dtype=np.float64) / half)).astype(np.float32)
    angles = np.arange(SEQ, dtype=np.float32)[:, None] * frequency[None, :]
    cosine, sine = np.cos(angles), np.sin(angles)
    return (
        np.concatenate([cosine, cosine], axis=1).astype(np.float32),
        np.concatenate([-sine, sine], axis=1).astype(np.float32),
    )


def dot(a, b, contract):
    return lax.dot_general(
        a, b, (((contract[0],), (contract[1],)), ((), ())), preferred_element_type=F32
    )


def turned(values, cosine, sine):
    return values * cosine + pltpu.roll(values, HEAD // 2, 1) * sine


def moved(weight, gradient, rate):
    gradient = gradient.astype(BF16).astype(F32)
    return (weight.astype(F32) - rate * gradient).astype(BF16)


def replica(z, y, core):
    return (z * Y_CHIPS + y) * 2 + core


def step_kernel(
    distance,
    x_in, cot_in, wq_in, wk_in, wv_in, wo_in, docs_in, cos_in, sin_in, rate_ref,
    layer_out, q_out, k_out, v_out, o_out,
    x_all, x_turned, cot, w_qkv, w_o, u_o, acc, d_mixed, dqkv, mixed_all, mixed_turned,
    docs, cos_ref, sin_ref, peer_o, peer_qkv, relay, partials, landed, across_sent, across_landed,
    send_sems, recv_sems, load_sems, o_sems, qkv_sems, relay_send, relay_recv,
    direct_send, direct_recv, sum_send, sum_recv, across_sems,
):
    me = lax.axis_index("tp")
    x, z = me % X_CHIPS, me // X_CHIPS
    right = z * X_CHIPS + (x + 1) % X_CHIPS
    left = z * X_CHIPS + (x + 3) % X_CHIPS
    far = z * X_CHIPS + (x + 2) % X_CHIPS
    across = (1 - z) * X_CHIPS + x
    across_right = (1 - z) * X_CHIPS + (x + 1) % X_CHIPS
    across_left = (1 - z) * X_CHIPS + (x + 3) % X_CHIPS
    across_far = (1 - z) * X_CHIPS + (x + 2) % X_CHIPS

    mine = lax.axis_index("rep")
    replicas = 2 * 2 * Y_CHIPS
    core, y, z_lo = mine % 2, mine // 2 % Y_CHIPS, mine // (2 * Y_CHIPS)
    target, origin = (mine + distance) % replicas, (mine + replicas - distance) % replicas
    around = distance <= 2
    back, ahead = (y + 3) % Y_CHIPS, (y + 1) % Y_CHIPS
    at_two, at_one = y // 2 * (1 - y % 2), (1 - y // 2) * (y % 2)
    hops_to = [
        replica(z_lo, back, core),
        replica((z_lo + at_two) % 2, back, core),
        replica(z_lo, back, core),
    ]
    hops_from = [
        replica(z_lo, ahead, core),
        replica((z_lo + at_one) % 2, ahead, core),
        replica(z_lo, ahead, core),
    ]
    if distance == 1:
        hops_to[2] = replica(z_lo, (y + 3 * core) % Y_CHIPS, 1 - core)
        hops_from[2] = replica(z_lo, (y + 1 - core) % Y_CHIPS, 1 - core)

    barrier = pltpu.get_barrier_semaphore()
    for peer in (left, right, far, across):
        pl.semaphore_signal(barrier, inc=1, device_id={"tp": peer}, device_id_type=MESH)
    senders = [origin] + (hops_from if around else [])
    for peer in senders:
        pl.semaphore_signal(barrier, inc=1, device_id={"rep": peer}, device_id_type=MESH)
    loads = [
        pltpu.make_async_copy(src, dst, load_sems.at[index])
        for index, (src, dst) in enumerate(
            (
                (cot_in, cot),
                (wo_in, w_o),
                (x_in, x_all.at[me]),
                (wq_in, w_qkv.at[:, pl.ds(0, Q_COLS)]),
                (wk_in, w_qkv.at[:, pl.ds(Q_COLS, HEAD)]),
                (wv_in, w_qkv.at[:, pl.ds(Q_COLS + HEAD, HEAD)]),
                (docs_in, docs),
                (cos_in, cos_ref),
                (sin_in, sin_ref),
            )
        )
    ]
    for load in loads[:2]:
        load.start()
    pl.semaphore_wait(barrier, 4 + len(senders))

    def remote(src, dst, peer, index):
        return pltpu.make_async_remote_copy(
            src_ref=src, dst_ref=dst, send_sem=send_sems.at[index], recv_sem=recv_sems.at[index],
            device_id={"tp": peer}, device_id_type=MESH,
        )

    upper, lower = pl.ds(0, TOKENS // 2), pl.ds(TOKENS // 2, TOKENS // 2)
    own = x_all.at[me]
    to_right = remote(x_in, own, right, 0)
    to_left = remote(x_in, own, left, 1)
    to_across = remote(x_in, own, across, 2)
    part = x_all.at[left, upper]
    far_right = remote(part, part, right, 3)
    part = x_all.at[right, lower]
    far_left = remote(part, part, left, 4)
    part = x_all.at[across]
    across_to_right = remote(part, part, right, 5)
    across_to_left = remote(part, part, left, 6)
    part = x_all.at[far]
    far_to_across = remote(part, part, across, 7)

    to_right.start()
    to_left.start()
    to_across.start()
    for load in loads[2:]:
        load.start()
    for load in loads[:2]:
        load.wait()

    acc[:, :Q_COLS] = jnp.zeros((TOKENS, Q_COLS), F32)

    @pl.loop(0, TP)
    def _(step):
        columns = pl.ds(pl.multiple_of(step * SLAB, SLAB), SLAB)
        acc[:, :Q_COLS] += dot(cot[:, columns], w_o[:, columns], (1, 1))

    d_mixed[...] = (acc[:, :Q_COLS] * SCALE).astype(BF16)

    for load in loads[2:]:
        load.wait()

    acc[...] = jnp.zeros((TOKENS, QKV), F32)
    order = (me, left, right, across, far, across_left, across_right, across_far)

    def on_step_1():
        to_right.wait_recv()
        far_right.start()
        to_left.wait_recv()
        far_left.start()

    def on_step_2():
        to_across.wait_recv()
        across_to_right.start()
        across_to_left.start()

    def on_step_3():
        far_right.wait_recv()
        far_left.wait_recv()
        far_to_across.start()

    arrivals = {
        1: on_step_1,
        2: on_step_2,
        3: on_step_3,
        5: across_to_right.wait_recv,
        6: across_to_left.wait_recv,
        7: far_to_across.wait_recv,
    }

    @pl.loop(0, TP)
    def _(turn):
        block = order[0]
        for index in range(1, TP):
            block = jnp.where(turn == index, order[index], block)
        for index, arrival in arrivals.items():
            pl.when(turn == index)(arrival)
        rows = pl.ds(pl.multiple_of(block * SLAB, SLAB), SLAB)

        @pl.loop(0, QKV // 256)
        def _(step):
            columns = pl.ds(pl.multiple_of(step * 256, 256), 256)
            acc[:, columns] += dot(x_all[block], w_qkv[rows, columns], (1, 0))

        x_turned[rows, :] = x_all[block].T

    cosine, sine = cos_ref[...], sin_ref[...]
    later = lax.broadcasted_iota(jnp.int32, (SEQ, SEQ), 0)
    earlier = lax.broadcasted_iota(jnp.int32, (SEQ, SEQ), 1)
    causal = earlier <= later
    heads = range(Q_HEADS)

    @pl.loop(0, SEQS)
    def _(sequence):
        rows = pl.ds(pl.multiple_of(sequence * SEQ, SEQ), SEQ)

        def stacked(pieces):
            return jnp.concatenate(pieces, axis=0)

        queries = stacked(
            [
                turned(acc[rows, h * HEAD : (h + 1) * HEAD] * SCALE, cosine, sine).astype(BF16)
                for h in heads
            ]
        )
        keys = turned(acc[rows, Q_COLS : Q_COLS + HEAD] * SCALE, cosine, sine).astype(BF16)
        values = (acc[rows, Q_COLS + HEAD :] * SCALE).astype(BF16)
        number = jnp.broadcast_to(docs[pl.ds(sequence, 1), :].astype(F32), (SEQ, SEQ))
        allowed = jnp.logical_and(causal, number == number.T)
        scores = dot(queries, keys, (1, 1)) * SCORE_SCALE
        scores = stacked(
            [jnp.where(allowed, scores[h * SEQ : (h + 1) * SEQ], -1e9) for h in heads]
        )
        exps = jnp.exp(scores - jnp.max(scores, axis=1, keepdims=True))
        probs = exps / jnp.sum(exps, axis=1, keepdims=True)
        rounded = probs.astype(BF16)
        mixed = dot(rounded, values, (1, 0)).astype(BF16)
        d_heads = stacked([d_mixed[rows, h * HEAD : (h + 1) * HEAD] for h in heads])
        d_probs = dot(d_heads, values, (1, 1)).astype(BF16).astype(F32)
        d_values = dot(rounded, d_heads, (0, 0)).astype(BF16)
        d_scores = probs * (d_probs - jnp.sum(d_probs * probs, axis=1, keepdims=True))
        d_scores = (d_scores * SCORE_SCALE).astype(BF16)
        d_queries = dot(d_scores, keys, (1, 0)).astype(BF16).astype(F32)
        d_keys = dot(d_scores, queries, (0, 0)).astype(BF16).astype(F32)
        for h in heads:
            columns = slice(h * HEAD, (h + 1) * HEAD)
            stack = slice(h * SEQ, (h + 1) * SEQ)
            mixed_all[rows, columns] = mixed[stack]
            mixed_turned[columns, rows] = mixed[stack].T
            dqkv[rows, columns] = (turned(d_queries[stack], cosine, -sine) * SCALE).astype(BF16)
        dqkv[rows, Q_COLS : Q_COLS + HEAD] = (turned(d_keys, cosine, -sine) * SCALE).astype(BF16)
        dqkv[rows, Q_COLS + HEAD :] = (d_values.astype(F32) * SCALE).astype(BF16)

    rate = rate_ref[0]
    top, bottom = pl.ds(0, DIRECT_ROWS), pl.ds(DIRECT_ROWS, AROUND_ROWS)
    direct_rows = top if around else pl.ds(0, Q_COLS)

    def o_columns(step):
        return pl.ds(pl.multiple_of(step * O_COLS, O_COLS), O_COLS)

    def qkv_rows(step):
        return pl.ds(pl.multiple_of(step * SLAB, SLAB), SLAB)

    def sent_to(src, dst, sems, index, peer):
        return pltpu.make_async_remote_copy(
            src_ref=src, dst_ref=dst, send_sem=sems[0].at[index], recv_sem=sems[1].at[index],
            device_id={"rep": peer}, device_id_type=MESH,
        )

    def direct_o(step):
        part = (direct_rows, o_columns(step))
        return sent_to(u_o.at[part], peer_o.at[part], (direct_send, direct_recv), step, target)

    def direct_qkv(step):
        rows = qkv_rows(step)
        return sent_to(
            w_qkv.at[rows, :], peer_qkv.at[rows, :],
            (direct_send, direct_recv), O_STEPS + step, target,
        )

    def relayed(hop, step, own=False):
        columns = o_columns(step)
        src = u_o.at[bottom, columns] if own or hop == 0 else relay.at[hop - 1, :, columns]
        dst = peer_o.at[bottom, columns] if hop == 2 else relay.at[hop, :, columns]
        return sent_to(src, dst, (relay_send, relay_recv), hop * O_STEPS + step, hops_to[hop])

    def relaying(action):
        if distance == 1:
            pl.when(core == 1)(action)
        else:
            action()

    @pl.loop(0, O_STEPS)
    def _(step):
        columns = o_columns(step)

        @pl.loop(0, O_COLS // SLAB)
        def _(half):
            piece = pl.ds(pl.multiple_of(step * O_COLS + half * SLAB, SLAB), SLAB)
            gradient = dot(mixed_turned[...], cot[:, piece], (1, 0)) * SCALE
            u_o[:, piece] = moved(w_o[:, piece], gradient, rate)
        if around:
            relaying(lambda: relayed(0, step).start())
        if distance == 1:
            pl.when(core == 0)(lambda: relayed(2, step, own=True).start())
        direct_o(step).start()

    @pl.loop(0, TP)
    def _(step):
        rows = qkv_rows(step)
        gradient = dot(x_turned[rows, :], dqkv[...], (1, 0))
        w_qkv[rows, :] = moved(w_qkv[rows, :], gradient, rate)

        @pl.when(step < WINDOW - O_STEPS)
        def _():
            direct_qkv(step).start()

    def partial(to_x, to_z, half):
        owner = to_z * X_CHIPS + to_x
        columns = pl.ds(pl.multiple_of(owner * SLAB + half * 256, 256), 256)
        return dot(mixed_all[...], w_o[:, columns], (1, 0)) * SCALE

    def half_slab(half):
        return pl.ds(pl.multiple_of(half * 256, 256), 256)

    def sum_copy(slot):
        to_x = (x + slot % 3 + 1) % X_CHIPS
        return pltpu.make_async_remote_copy(
            src_ref=partials.at[slot], dst_ref=landed.at[slot],
            send_sem=sum_send.at[slot], recv_sem=sum_recv.at[slot],
            device_id={"tp": z * X_CHIPS + to_x}, device_id_type=MESH,
        )

    @pl.loop(0, 6)
    def _(slot):
        to_x = (x + slot % 3 + 1) % X_CHIPS
        to_z = (z + 1 + slot // 3) % 2

        @pl.loop(0, 2)
        def _(half):
            partials[slot, :, half_slab(half)] = partial(to_x, to_z, half).astype(BF16)

        sum_copy(slot).start()

    def summed(plane, to_z, into, extra=None):
        for slot in range(plane * 3, plane * 3 + 3):
            sum_copy(slot).wait_recv()

        @pl.loop(0, 2)
        def _(half):
            columns = half_slab(half)
            total = partial(x, to_z, half)
            for slot in range(plane * 3, plane * 3 + 3):
                total += landed[slot, :, columns].astype(F32)
            if extra is not None:
                total += extra[:, columns].astype(F32)
            into[:, columns] = total.astype(BF16)

    crossing = pltpu.make_async_remote_copy(
        src_ref=across_sent, dst_ref=across_landed,
        send_sem=across_sems.at[0], recv_sem=across_sems.at[1],
        device_id={"tp": across}, device_id_type=MESH,
    )

    def cross():
        summed(0, 1 - z, across_sent)
        crossing.start()

    def finish_output():
        crossing.wait_recv()
        summed(1, z, layer_out, across_landed)

    def averaged(own, peer, first_row, rows, columns):
        @pl.loop(0, rows // 16)
        def _(step):
            part = pl.ds(pl.multiple_of(first_row + step * 16, 16), 16)
            total = own[part, columns].astype(F32) + peer[part, columns].astype(F32)
            peer[part, columns] = (0.5 * total).astype(BF16)

    def store_o(step, index, rows):
        part = (rows, o_columns(step))
        return pltpu.make_async_copy(peer_o.at[part], o_out.at[part], o_sems.at[step, index])

    def stores_qkv(step):
        rows = qkv_rows(step)
        return [
            pltpu.make_async_copy(
                peer_qkv.at[rows, pl.ds(start, out.shape[1])], out.at[rows, :],
                qkv_sems.at[step, index],
            )
            for index, (start, out) in enumerate(
                ((0, q_out), (Q_COLS, k_out), (Q_COLS + HEAD, v_out))
            )
        ]

    def arrived(index):
        if index + WINDOW < O_STEPS + TP:
            direct_qkv(index + WINDOW - O_STEPS).start()
        if index < O_STEPS:
            direct_o(index).wait_recv()
            averaged(u_o, peer_o, 0, DIRECT_ROWS if around else Q_COLS, o_columns(index))
            store_o(index, 0, direct_rows).start()
        else:
            step = index - O_STEPS
            direct_qkv(step).wait_recv()
            averaged(w_qkv, peer_qkv, step * SLAB, SLAB, slice(None))
            for store in stores_qkv(step):
                store.start()

    def pass_on(hop):
        def action():
            @pl.loop(0, O_STEPS)
            def _(step):
                relayed(hop - 1, step).wait_recv()
                relayed(hop, step).start()

        relaying(action)

    events = {
        1: {4: [lambda: pass_on(1)], 7: [cross, lambda: pass_on(2)]},
        2: {4: [lambda: pass_on(1), cross], 7: [lambda: pass_on(2)]},
        4: {1: [cross]},
        8: {1: [cross]},
    }[distance]
    for index in range(O_STEPS + TP):
        arrived(index)
        for event in events.get(index, ()):
            event()

    finish_output()
    if around:
        for step in range(O_STEPS):
            relayed(2, step).wait_recv()
            averaged(u_o, peer_o, DIRECT_ROWS, AROUND_ROWS, o_columns(step))
            store_o(step, 1, bottom).start()

    for step in range(O_STEPS):
        direct_o(step).wait_send()
        store_o(step, 0, direct_rows).wait()
        if around:
            store_o(step, 1, bottom).wait()
            relayed(2, step).wait_send()
    for step in range(TP):
        direct_qkv(step).wait_send()
        for store in stores_qkv(step):
            store.wait()
    if around:

        def relays_sent():
            for step in range(O_STEPS):
                relayed(0, step).wait_send()
                relayed(1, step).wait_send()

        relaying(relays_sent)
    for copy in (
        to_right, to_left, to_across, far_right, far_left,
        across_to_right, across_to_left, far_to_across, *map(sum_copy, range(6)), crossing,
    ):
        copy.wait_send()


def step(distance, normed, cotangent, w_query, w_key, w_value, w_out, documents, rate):
    cosine, sine = rotation_tables()
    hbm = pl.BlockSpec(memory_space=pl.ANY)
    vmem = pl.BlockSpec(memory_space=pltpu.VMEM)
    dma = pltpu.SemaphoreType.DMA
    block = (TOKENS, SLAB)
    layer_out, *new = pl.pallas_call(
        functools.partial(step_kernel, distance),
        name="step_%d" % distance,
        out_shape=(
            jax.ShapeDtypeStruct(block, BF16),
            jax.ShapeDtypeStruct((D, Q_COLS), BF16),
            jax.ShapeDtypeStruct((D, HEAD), BF16),
            jax.ShapeDtypeStruct((D, HEAD), BF16),
            jax.ShapeDtypeStruct((Q_COLS, D), BF16),
        ),
        in_specs=[hbm] * 9 + [pl.BlockSpec(memory_space=pltpu.SMEM)],
        out_specs=(vmem, hbm, hbm, hbm, hbm),
        scratch_shapes=[
            pltpu.VMEM((TP, TOKENS, SLAB), BF16),
            pltpu.VMEM((D, TOKENS), BF16),
            pltpu.VMEM((TOKENS, D), BF16),
            pltpu.VMEM((D, QKV), BF16),
            pltpu.VMEM((Q_COLS, D), BF16),
            pltpu.VMEM((Q_COLS, D), BF16),
            pltpu.VMEM((TOKENS, QKV), F32),
            pltpu.VMEM((TOKENS, Q_COLS), BF16),
            pltpu.VMEM((TOKENS, QKV), BF16),
            pltpu.VMEM((TOKENS, Q_COLS), BF16),
            pltpu.VMEM((Q_COLS, TOKENS), BF16),
            pltpu.VMEM((SEQS, SEQ), jnp.int32),
            pltpu.VMEM((SEQ, HEAD), F32),
            pltpu.VMEM((SEQ, HEAD), F32),
            pltpu.VMEM((Q_COLS, D), BF16),
            pltpu.VMEM((D, QKV), BF16),
            pltpu.VMEM((2, AROUND_ROWS, D), BF16) if distance <= 2 else pltpu.VMEM((2, 16, 128), BF16),
            pltpu.VMEM((6, *block), BF16),
            pltpu.VMEM((6, *block), BF16),
            pltpu.VMEM(block, BF16),
            pltpu.VMEM(block, BF16),
            dma((8,)),
            dma((8,)),
            dma((9,)),
            dma((O_STEPS, 2)),
            dma((TP, 3)),
            dma((3 * O_STEPS,)),
            dma((3 * O_STEPS,)),
            dma((O_STEPS + TP,)),
            dma((O_STEPS + TP,)),
            dma((6,)),
            dma((6,)),
            dma((2,)),
        ],
        compiler_params=pltpu.CompilerParams(
            collective_id=distance, has_side_effects=True, vmem_limit_bytes=62 * 1024 * 1024
        ),
        cost_estimate=pl.CostEstimate(
            flops=14_000_000_000, bytes_accessed=30_000_000, transcendentals=300_000
        ),
    )(normed, cotangent, w_query, w_key, w_value, w_out, documents, cosine, sine, rate)
    return (layer_out.reshape(SEQS, SEQ, SLAB), *(n[None] for n in new))


def per_device(normed, documents, cotangent, w_query, w_key, w_value, w_out, step_index):
    levels = lax.axis_size("rep").bit_length() - 1
    level = step_index[0] % levels
    rate = 3.0 * 32.0 / (32.0 + step_index.astype(F32))
    return lax.switch(
        level,
        [functools.partial(step, 2**exponent) for exponent in range(levels)],
        normed.reshape(TOKENS, SLAB), cotangent.reshape(TOKENS, D),
        w_query[0], w_key[0], w_value[0], w_out[0], documents, rate,
    )


def solution(mesh):
    in_specs = (
        P("rep", None, "tp"),
        P("rep", None),
        P("rep", None, None),
        P("rep", None, "tp"),
        P("rep", None, "tp"),
        P("rep", None, "tp"),
        P("rep", "tp", None),
        P(),
    )
    out_specs = (
        P("rep", None, "tp"),
        P("rep", None, "tp"),
        P("rep", None, "tp"),
        P("rep", None, "tp"),
        P("rep", "tp", None),
    )
    return jax.shard_map(
        per_device, mesh=mesh, in_specs=in_specs, out_specs=out_specs, check_vma=False
    )
```

```python
import functools
import math

import jax
import jax.numpy as jnp
import numpy as np
from jax import lax
from jax.experimental import pallas as pl
from jax.experimental.pallas import tpu as pltpu
from jax.sharding import PartitionSpec as P

HEAD = 128
SEQS = 4
SEQ = 128
TOKENS = SEQS * SEQ
X_CHIPS = 4
Y_CHIPS = 4
TP = 8
D = 4096
SLAB = D // TP
Q_HEADS = 4
Q_COLS = Q_HEADS * HEAD
QKV = Q_COLS + 2 * HEAD
DIRECT_ROWS = 192
AROUND_ROWS = Q_COLS - DIRECT_ROWS
O_STEPS = 4
O_COLS = D // O_STEPS
WINDOW = 6
CROSSINGS = 8
CROSSING_ROWS = TOKENS // CROSSINGS
DETOURS = {1: 1, 2: 1, 4: 3, 8: 0}
SCALE = 1.0 / math.sqrt(D)
SCORE_SCALE = 1.0 / math.sqrt(HEAD)
MESH = pl.DeviceIdType.MESH
F32 = jnp.float32
BF16 = jnp.bfloat16


def rotation_tables():
    half = HEAD // 2
    frequency = (500000.0 ** (-np.arange(half, dtype=np.float64) / half)).astype(np.float32)
    angles = np.arange(SEQ, dtype=np.float32)[:, None] * frequency[None, :]
    cosine, sine = np.cos(angles), np.sin(angles)
    return (
        np.concatenate([cosine, cosine], axis=1).astype(np.float32),
        np.concatenate([-sine, sine], axis=1).astype(np.float32),
    )


def dot(a, b, contract):
    return lax.dot_general(
        a, b, (((contract[0],), (contract[1],)), ((), ())), preferred_element_type=F32
    )


def turned(values, cosine, sine):
    return values * cosine + pltpu.roll(values, HEAD // 2, 1) * sine


def moved(weight, gradient, rate):
    gradient = gradient.astype(BF16).astype(F32)
    return (weight.astype(F32) - rate * gradient).astype(BF16)


def replica(z, y, core):
    return (z * Y_CHIPS + y) * 2 + core


def step_kernel(
    distance,
    x_in, cot_in, wq_in, wk_in, wv_in, wo_in, docs_in, cos_in, sin_in, rate_ref,
    layer_out, qkv_out, o_out,
    x_all, x_turned, cot, w_qkv, w_o, u_o, acc, d_mixed, dqkv, mixed_all, mixed_turned,
    docs, cos_ref, sin_ref, peer_o, peer_qkv, relay, partials, landed, across_sent, across_landed,
    send_sems, recv_sems, load_sems, o_sems, qkv_sems, relay_send, relay_recv,
    direct_send, direct_recv, sum_send, sum_recv, across_sems, detour, detour_sems,
):
    me = lax.axis_index("tp")
    x, z = me % X_CHIPS, me // X_CHIPS
    right = z * X_CHIPS + (x + 1) % X_CHIPS
    left = z * X_CHIPS + (x + 3) % X_CHIPS
    far = z * X_CHIPS + (x + 2) % X_CHIPS
    across = (1 - z) * X_CHIPS + x
    across_right = (1 - z) * X_CHIPS + (x + 1) % X_CHIPS
    across_left = (1 - z) * X_CHIPS + (x + 3) % X_CHIPS
    across_far = (1 - z) * X_CHIPS + (x + 2) % X_CHIPS

    mine = lax.axis_index("rep")
    replicas = 2 * 2 * Y_CHIPS
    core, y, z_lo = mine % 2, mine // 2 % Y_CHIPS, mine // (2 * Y_CHIPS)
    target, origin = (mine + distance) % replicas, (mine + replicas - distance) % replicas
    around = distance <= 2
    back, ahead = (y + 3) % Y_CHIPS, (y + 1) % Y_CHIPS
    at_two, at_one = y // 2 * (1 - y % 2), (1 - y // 2) * (y % 2)
    hops_to = [
        replica(z_lo, back, core),
        replica((z_lo + at_two) % 2, back, core),
        replica(z_lo, back, core),
    ]
    hops_from = [
        replica(z_lo, ahead, core),
        replica((z_lo + at_one) % 2, ahead, core),
        replica(z_lo, ahead, core),
    ]
    if distance == 1:
        hops_to[2] = replica(z_lo, (y + 3 * core) % Y_CHIPS, 1 - core)
        hops_from[2] = replica(z_lo, (y + 1 - core) % Y_CHIPS, 1 - core)

    detours = DETOURS[distance]
    wraps = y + distance // 2 >= Y_CHIPS
    beside = replica(1 - z_lo, y, core)
    ahead_to = replica(z_lo, (y + distance // 2) % Y_CHIPS, core)
    ahead_from = replica(z_lo, (y + Y_CHIPS - distance // 2) % Y_CHIPS, core)

    if distance == 1:
        wraps = jnp.logical_and(y == Y_CHIPS - 1, core == 1)
        ahead_to = replica(z_lo, (y + core) % Y_CHIPS, 1 - core)
        ahead_from = replica(z_lo, (y + 3 * (1 - core)) % Y_CHIPS, 1 - core)

    barrier = pltpu.get_barrier_semaphore()
    for peer in (left, right, far, across):
        pl.semaphore_signal(barrier, inc=1, device_id={"tp": peer}, device_id_type=MESH)
    senders = [origin] + (hops_from if around else []) + ([beside, ahead_from] if detours else [])
    for peer in senders:
        pl.semaphore_signal(barrier, inc=1, device_id={"rep": peer}, device_id_type=MESH)
    loads = [
        pltpu.make_async_copy(src, dst, load_sems.at[index])
        for index, (src, dst) in enumerate(
            (
                (cot_in, cot),
                (wo_in, w_o),
                (x_in, x_all.at[me]),
                (wq_in, w_qkv.at[:, pl.ds(0, Q_COLS)]),
                (wk_in, w_qkv.at[:, pl.ds(Q_COLS, HEAD)]),
                (wv_in, w_qkv.at[:, pl.ds(Q_COLS + HEAD, HEAD)]),
                (docs_in, docs),
                (cos_in, cos_ref),
                (sin_in, sin_ref),
            )
        )
    ]
    for load in loads[:2]:
        load.start()
    pl.semaphore_wait(barrier, 4 + len(senders))

    def remote(src, dst, peer, index):
        return pltpu.make_async_remote_copy(
            src_ref=src, dst_ref=dst, send_sem=send_sems.at[index], recv_sem=recv_sems.at[index],
            device_id={"tp": peer}, device_id_type=MESH,
        )

    upper, lower = pl.ds(0, TOKENS // 2), pl.ds(TOKENS // 2, TOKENS // 2)
    own = x_all.at[me]
    to_right = remote(x_in, own, right, 0)
    to_left = remote(x_in, own, left, 1)
    to_across = remote(x_in, own, across, 2)
    part = x_all.at[left, upper]
    far_right = remote(part, part, right, 3)
    part = x_all.at[right, lower]
    far_left = remote(part, part, left, 4)
    part = x_all.at[across]
    across_to_right = remote(part, part, right, 5)
    across_to_left = remote(part, part, left, 6)
    part = x_all.at[far]
    far_to_across = remote(part, part, across, 7)

    to_right.start()
    to_left.start()
    to_across.start()
    for load in loads[2:]:
        load.start()
    for load in loads[:2]:
        load.wait()

    acc[:, :Q_COLS] = jnp.zeros((TOKENS, Q_COLS), F32)

    @pl.loop(0, TP)
    def _(step):
        columns = pl.ds(pl.multiple_of(step * SLAB, SLAB), SLAB)
        acc[:, :Q_COLS] += dot(cot[:, columns], w_o[:, columns], (1, 1))

    d_mixed[...] = (acc[:, :Q_COLS] * SCALE).astype(BF16)

    for load in loads[2:]:
        load.wait()

    acc[...] = jnp.zeros((TOKENS, QKV), F32)
    order = (me, left, right, across, far, across_left, across_right, across_far)

    def on_step_1():
        to_right.wait_recv()
        far_right.start()
        to_left.wait_recv()
        far_left.start()

    def on_step_2():
        to_across.wait_recv()
        across_to_right.start()
        across_to_left.start()

    def on_step_3():
        far_right.wait_recv()
        far_left.wait_recv()
        far_to_across.start()

    arrivals = {
        1: on_step_1,
        2: on_step_2,
        3: on_step_3,
        5: across_to_right.wait_recv,
        6: across_to_left.wait_recv,
        7: far_to_across.wait_recv,
    }

    @pl.loop(0, TP)
    def _(turn):
        block = order[0]
        for index in range(1, TP):
            block = jnp.where(turn == index, order[index], block)
        for index, arrival in arrivals.items():
            pl.when(turn == index)(arrival)
        rows = pl.ds(pl.multiple_of(block * SLAB, SLAB), SLAB)

        @pl.loop(0, QKV // 256)
        def _(step):
            columns = pl.ds(pl.multiple_of(step * 256, 256), 256)
            acc[:, columns] += dot(x_all[block], w_qkv[rows, columns], (1, 0))

        x_turned[rows, :] = x_all[block].T

    cosine, sine = cos_ref[...], sin_ref[...]
    later = lax.broadcasted_iota(jnp.int32, (SEQ, SEQ), 0)
    earlier = lax.broadcasted_iota(jnp.int32, (SEQ, SEQ), 1)
    causal = earlier <= later
    heads = range(Q_HEADS)

    @pl.loop(0, SEQS)
    def _(sequence):
        rows = pl.ds(pl.multiple_of(sequence * SEQ, SEQ), SEQ)

        def stacked(pieces):
            return jnp.concatenate(pieces, axis=0)

        queries = stacked(
            [
                turned(acc[rows, h * HEAD : (h + 1) * HEAD] * SCALE, cosine, sine).astype(BF16)
                for h in heads
            ]
        )
        keys = turned(acc[rows, Q_COLS : Q_COLS + HEAD] * SCALE, cosine, sine).astype(BF16)
        values = (acc[rows, Q_COLS + HEAD :] * SCALE).astype(BF16)
        number = jnp.broadcast_to(docs[pl.ds(sequence, 1), :].astype(F32), (SEQ, SEQ))
        allowed = jnp.logical_and(causal, number == number.T)
        scores = dot(queries, keys, (1, 1)) * SCORE_SCALE
        scores = stacked(
            [jnp.where(allowed, scores[h * SEQ : (h + 1) * SEQ], -1e9) for h in heads]
        )
        exps = jnp.exp(scores - jnp.max(scores, axis=1, keepdims=True))
        probs = exps / jnp.sum(exps, axis=1, keepdims=True)
        rounded = probs.astype(BF16)
        mixed = dot(rounded, values, (1, 0)).astype(BF16)
        d_heads = stacked([d_mixed[rows, h * HEAD : (h + 1) * HEAD] for h in heads])
        d_probs = dot(d_heads, values, (1, 1)).astype(BF16).astype(F32)
        d_values = dot(rounded, d_heads, (0, 0)).astype(BF16)
        d_scores = probs * (d_probs - jnp.sum(d_probs * probs, axis=1, keepdims=True))
        d_scores = (d_scores * SCORE_SCALE).astype(BF16)
        d_queries = dot(d_scores, keys, (1, 0)).astype(BF16).astype(F32)
        d_keys = dot(d_scores, queries, (0, 0)).astype(BF16).astype(F32)
        for h in heads:
            columns = slice(h * HEAD, (h + 1) * HEAD)
            stack = slice(h * SEQ, (h + 1) * SEQ)
            mixed_all[rows, columns] = mixed[stack]
            mixed_turned[columns, rows] = mixed[stack].T
            dqkv[rows, columns] = (turned(d_queries[stack], cosine, -sine) * SCALE).astype(BF16)
        dqkv[rows, Q_COLS : Q_COLS + HEAD] = (turned(d_keys, cosine, -sine) * SCALE).astype(BF16)
        dqkv[rows, Q_COLS + HEAD :] = (d_values.astype(F32) * SCALE).astype(BF16)

    rate = rate_ref[0]
    top, bottom = pl.ds(0, DIRECT_ROWS), pl.ds(DIRECT_ROWS, AROUND_ROWS)
    direct_rows = top if around else pl.ds(0, Q_COLS)

    def o_columns(step):
        return pl.ds(pl.multiple_of(step * O_COLS, O_COLS), O_COLS)

    def qkv_rows(step):
        return pl.ds(pl.multiple_of(step * SLAB, SLAB), SLAB)

    def sent_to(src, dst, sems, index, peer):
        return pltpu.make_async_remote_copy(
            src_ref=src, dst_ref=dst, send_sem=sems[0].at[index], recv_sem=sems[1].at[index],
            device_id={"rep": peer}, device_id_type=MESH,
        )

    def direct_o(step):
        part = (direct_rows, o_columns(step))
        return sent_to(u_o.at[part], peer_o.at[part], (direct_send, direct_recv), step, target)

    def direct_qkv(step):
        rows = qkv_rows(step)
        return sent_to(
            w_qkv.at[rows, :], peer_qkv.at[rows, :],
            (direct_send, direct_recv), O_STEPS + step, target,
        )

    def detoured(step):
        sems = (detour_sems.at[0], detour_sems.at[1])
        return sent_to(w_qkv.at[qkv_rows(step), :], detour.at[step], sems, step, beside)

    def handed_on(step):
        return sent_to(
            detour.at[step], peer_qkv.at[qkv_rows(step), :],
            (direct_send, direct_recv), O_STEPS + step, ahead_to,
        )

    def start_qkv(step):
        if step < detours:
            pl.when(wraps)(detoured(step).start)
            pl.when(jnp.logical_not(wraps))(direct_qkv(step).start)
        else:
            direct_qkv(step).start()

    def hand_on(*steps):
        def action():
            for step in steps:
                detoured(step).wait_recv()
                handed_on(step).start()

        pl.when(wraps)(action)

    def relayed(hop, step, own=False):
        columns = o_columns(step)
        src = u_o.at[bottom, columns] if own or hop == 0 else relay.at[hop - 1, :, columns]
        dst = peer_o.at[bottom, columns] if hop == 2 else relay.at[hop, :, columns]
        return sent_to(src, dst, (relay_send, relay_recv), hop * O_STEPS + step, hops_to[hop])

    def relaying(action):
        if distance == 1:
            pl.when(core == 1)(action)
        else:
            action()

    @pl.loop(0, O_STEPS)
    def _(step):
        columns = o_columns(step)

        @pl.loop(0, O_COLS // SLAB)
        def _(half):
            piece = pl.ds(pl.multiple_of(step * O_COLS + half * SLAB, SLAB), SLAB)
            gradient = dot(mixed_turned[...], cot[:, piece], (1, 0)) * SCALE
            u_o[:, piece] = moved(w_o[:, piece], gradient, rate)
        if around:
            relaying(lambda: relayed(0, step).start())
        if distance == 1:
            pl.when(core == 0)(lambda: relayed(2, step, own=True).start())
        direct_o(step).start()

    @pl.loop(0, TP)
    def _(step):
        rows = qkv_rows(step)
        gradient = dot(x_turned[rows, :], dqkv[...], (1, 0))
        w_qkv[rows, :] = moved(w_qkv[rows, :], gradient, rate)

    for step in range(detours + WINDOW - O_STEPS):
        start_qkv(step)

    def partial(to_x, to_z, half):
        owner = to_z * X_CHIPS + to_x
        columns = pl.ds(pl.multiple_of(owner * SLAB + half * 256, 256), 256)
        return dot(mixed_all[...], w_o[:, columns], (1, 0)) * SCALE

    def half_slab(half):
        return pl.ds(pl.multiple_of(half * 256, 256), 256)

    def sum_copy(slot):
        to_x = (x + slot % 3 + 1) % X_CHIPS
        return pltpu.make_async_remote_copy(
            src_ref=partials.at[slot], dst_ref=landed.at[slot],
            send_sem=sum_send.at[slot], recv_sem=sum_recv.at[slot],
            device_id={"tp": z * X_CHIPS + to_x}, device_id_type=MESH,
        )

    @pl.loop(0, 6)
    def _(slot):
        to_x = (x + slot % 3 + 1) % X_CHIPS
        to_z = (z + 1 + slot // 3) % 2

        @pl.loop(0, 2)
        def _(half):
            partials[slot, :, half_slab(half)] = partial(to_x, to_z, half).astype(BF16)

        sum_copy(slot).start()

    def summed(plane, to_z, into, extra=None):
        for slot in range(plane * 3, plane * 3 + 3):
            sum_copy(slot).wait_recv()

        @pl.loop(0, 2)
        def _(half):
            columns = half_slab(half)
            total = partial(x, to_z, half)
            for slot in range(plane * 3, plane * 3 + 3):
                total += landed[slot, :, columns].astype(F32)
            if extra is not None:
                total += extra[:, columns].astype(F32)
            into[:, columns] = total.astype(BF16)

    def crossing(part):
        rows = pl.ds(part * CROSSING_ROWS, CROSSING_ROWS)
        return pltpu.make_async_remote_copy(
            src_ref=across_sent.at[rows, :], dst_ref=across_landed.at[rows, :],
            send_sem=across_sems.at[0, part], recv_sem=across_sems.at[1, part],
            device_id={"tp": across}, device_id_type=MESH,
        )

    crossings = [crossing(part) for part in range(CROSSINGS)]

    def cross():
        summed(0, 1 - z, across_sent)
        for copy in crossings:
            copy.start()

    def finish_output():
        for copy in crossings:
            copy.wait_recv()
        summed(1, z, layer_out, across_landed)

    def averaged(own, peer, first_row, rows, columns):
        @pl.loop(0, rows // 16)
        def _(step):
            part = pl.ds(pl.multiple_of(first_row + step * 16, 16), 16)
            total = own[part, columns].astype(F32) + peer[part, columns].astype(F32)
            peer[part, columns] = (0.5 * total).astype(BF16)

    def store_o(step, index, rows):
        part = (rows, o_columns(step))
        return pltpu.make_async_copy(peer_o.at[part], o_out.at[part], o_sems.at[step, index])

    def store_qkv(step):
        rows = qkv_rows(step)
        return pltpu.make_async_copy(peer_qkv.at[rows, :], qkv_out.at[rows, :], qkv_sems.at[step])

    def arrived(index):
        if index + detours + WINDOW < O_STEPS + TP:
            start_qkv(index + detours + WINDOW - O_STEPS)
        if index < O_STEPS:
            direct_o(index).wait_recv()
            averaged(u_o, peer_o, 0, DIRECT_ROWS if around else Q_COLS, o_columns(index))
            store_o(index, 0, direct_rows).start()
        else:
            step = (index - O_STEPS + detours) % TP
            direct_qkv(step).wait_recv()
            averaged(w_qkv, peer_qkv, step * SLAB, SLAB, slice(None))
            store_qkv(step).start()

    def pass_on(hop):
        def action():
            @pl.loop(0, O_STEPS)
            def _(step):
                relayed(hop - 1, step).wait_recv()
                relayed(hop, step).start()

        relaying(action)

    events = {
        1: {2: [lambda: hand_on(0)], 4: [lambda: pass_on(1)], 7: [cross, lambda: pass_on(2)]},
        2: {
            1: [lambda: hand_on(0)],
            4: [lambda: pass_on(1), cross],
            7: [lambda: pass_on(2)],
        },
        4: {1: [lambda: hand_on(0), cross], 2: [lambda: hand_on(1, 2)]},
        8: {1: [cross]},
    }[distance]
    for index in range(O_STEPS + TP):
        arrived(index)
        for event in events.get(index, ()):
            event()

    finish_output()
    if around:
        for step in range(O_STEPS):
            relayed(2, step).wait_recv()
            averaged(u_o, peer_o, DIRECT_ROWS, AROUND_ROWS, o_columns(step))
            store_o(step, 1, bottom).start()

    for step in range(O_STEPS):
        direct_o(step).wait_send()
        store_o(step, 0, direct_rows).wait()
        if around:
            store_o(step, 1, bottom).wait()
            relayed(2, step).wait_send()
    for step in range(TP):
        direct_qkv(step).wait_send()
        store_qkv(step).wait()
    for step in range(detours):
        pl.when(wraps)(detoured(step).wait_send)
    if around:

        def relays_sent():
            for step in range(O_STEPS):
                relayed(0, step).wait_send()
                relayed(1, step).wait_send()

        relaying(relays_sent)
    for copy in (
        to_right, to_left, to_across, far_right, far_left,
        across_to_right, across_to_left, far_to_across, *map(sum_copy, range(6)), *crossings,
    ):
        copy.wait_send()


def step(distance, normed, cotangent, w_query, w_key, w_value, w_out, documents, rate):
    cosine, sine = rotation_tables()
    hbm = pl.BlockSpec(memory_space=pl.ANY)
    vmem = pl.BlockSpec(memory_space=pltpu.VMEM)
    dma = pltpu.SemaphoreType.DMA
    block = (TOKENS, SLAB)
    layer_out, new_qkv, new_o = pl.pallas_call(
        functools.partial(step_kernel, distance),
        name="step_%d" % distance,
        out_shape=(
            jax.ShapeDtypeStruct(block, BF16),
            jax.ShapeDtypeStruct((D, QKV), BF16),
            jax.ShapeDtypeStruct((Q_COLS, D), BF16),
        ),
        in_specs=[hbm] * 9 + [pl.BlockSpec(memory_space=pltpu.SMEM)],
        out_specs=(vmem, hbm, hbm),
        scratch_shapes=[
            pltpu.VMEM((TP, TOKENS, SLAB), BF16),
            pltpu.VMEM((D, TOKENS), BF16),
            pltpu.VMEM((TOKENS, D), BF16),
            pltpu.VMEM((D, QKV), BF16),
            pltpu.VMEM((Q_COLS, D), BF16),
            pltpu.VMEM((Q_COLS, D), BF16),
            pltpu.VMEM((TOKENS, QKV), F32),
            pltpu.VMEM((TOKENS, Q_COLS), BF16),
            pltpu.VMEM((TOKENS, QKV), BF16),
            pltpu.VMEM((TOKENS, Q_COLS), BF16),
            pltpu.VMEM((Q_COLS, TOKENS), BF16),
            pltpu.VMEM((SEQS, SEQ), jnp.int32),
            pltpu.VMEM((SEQ, HEAD), F32),
            pltpu.VMEM((SEQ, HEAD), F32),
            pltpu.VMEM((Q_COLS, D), BF16),
            pltpu.VMEM((D, QKV), BF16),
            pltpu.VMEM((2, AROUND_ROWS, D), BF16) if distance <= 2 else pltpu.VMEM((2, 16, 128), BF16),
            pltpu.VMEM((6, *block), BF16),
            pltpu.VMEM((6, *block), BF16),
            pltpu.VMEM(block, BF16),
            pltpu.VMEM(block, BF16),
            dma((8,)),
            dma((8,)),
            dma((9,)),
            dma((O_STEPS, 2)),
            dma((TP,)),
            dma((3 * O_STEPS,)),
            dma((3 * O_STEPS,)),
            dma((O_STEPS + TP,)),
            dma((O_STEPS + TP,)),
            dma((6,)),
            dma((6,)),
            dma((2, CROSSINGS)),
            pltpu.VMEM((DETOURS[distance], SLAB, QKV) if DETOURS[distance] else (1, 16, 128), BF16),
            dma((2, max(1, DETOURS[distance]))),
        ],
        compiler_params=pltpu.CompilerParams(
            collective_id=distance, has_side_effects=True, vmem_limit_bytes=62 * 1024 * 1024
        ),
        cost_estimate=pl.CostEstimate(
            flops=14_000_000_000, bytes_accessed=30_000_000, transcendentals=300_000
        ),
    )(normed, cotangent, w_query, w_key, w_value, w_out, documents, cosine, sine, rate)
    new = (
        new_qkv[:, :Q_COLS], new_qkv[:, Q_COLS : Q_COLS + HEAD], new_qkv[:, Q_COLS + HEAD :], new_o
    )
    return (layer_out.reshape(SEQS, SEQ, SLAB), *(n[None] for n in new))


def per_device(normed, documents, cotangent, w_query, w_key, w_value, w_out, step_index):
    levels = lax.axis_size("rep").bit_length() - 1
    level = step_index[0] % levels
    rate = 3.0 * 32.0 / (32.0 + step_index.astype(F32))
    return lax.switch(
        level,
        [functools.partial(step, 2**exponent) for exponent in range(levels)],
        normed.reshape(TOKENS, SLAB), cotangent.reshape(TOKENS, D),
        w_query[0], w_key[0], w_value[0], w_out[0], documents, rate,
    )


def solution(mesh):
    in_specs = (
        P("rep", None, "tp"),
        P("rep", None),
        P("rep", None, None),
        P("rep", None, "tp"),
        P("rep", None, "tp"),
        P("rep", None, "tp"),
        P("rep", "tp", None),
        P(),
    )
    out_specs = (
        P("rep", None, "tp"),
        P("rep", None, "tp"),
        P("rep", None, "tp"),
        P("rep", None, "tp"),
        P("rep", "tp", None),
    )
    return jax.shard_map(
        per_device, mesh=mesh, in_specs=in_specs, out_specs=out_specs, check_vma=False
    )
```

```python
import functools
import math

import jax
import jax.numpy as jnp
import numpy as np
from jax import lax
from jax.experimental import pallas as pl
from jax.experimental.pallas import tpu as pltpu
from jax.sharding import PartitionSpec as P

HEAD = 128
SEQS = 4
SEQ = 128
TOKENS = SEQS * SEQ
X_CHIPS = 4
Y_CHIPS = 4
TP = 8
D = 4096
SLAB = D // TP
Q_HEADS = 4
Q_COLS = Q_HEADS * HEAD
QKV = Q_COLS + 2 * HEAD
DIRECT_ROWS = 192
AROUND_ROWS = Q_COLS - DIRECT_ROWS
O_STEPS = 4
O_COLS = D // O_STEPS
WINDOW = 6
CROSSINGS = 8
CROSSING_ROWS = TOKENS // CROSSINGS
DETOURS = {1: 1, 2: 1, 4: 3, 8: 0}
SCALE = 1.0 / math.sqrt(D)
SCORE_SCALE = 1.0 / math.sqrt(HEAD)
MESH = pl.DeviceIdType.MESH
F32 = jnp.float32
BF16 = jnp.bfloat16


def rotation_tables():
    half = HEAD // 2
    frequency = (500000.0 ** (-np.arange(half, dtype=np.float64) / half)).astype(np.float32)
    angles = np.arange(SEQ, dtype=np.float32)[:, None] * frequency[None, :]
    cosine, sine = np.cos(angles), np.sin(angles)
    return (
        np.concatenate([cosine, cosine], axis=1).astype(np.float32),
        np.concatenate([-sine, sine], axis=1).astype(np.float32),
    )


def dot(a, b, contract):
    return lax.dot_general(
        a, b, (((contract[0],), (contract[1],)), ((), ())), preferred_element_type=F32
    )


def turned(values, cosine, sine):
    return values * cosine + pltpu.roll(values, HEAD // 2, 1) * sine


def moved(weight, gradient, rate):
    gradient = gradient.astype(BF16).astype(F32)
    return (weight.astype(F32) - rate * gradient).astype(BF16)


def replica(z, y, core):
    return (z * Y_CHIPS + y) * 2 + core


def step_kernel(
    distance,
    x_in, cot_in, wq_in, wk_in, wv_in, wo_in, docs_in, cos_in, sin_in, rate_ref,
    layer_out, qkv_out, o_out,
    x_all, x_turned, cot, w_qkv, w_o, u_o, acc, d_mixed, dqkv, mixed_all, mixed_turned,
    docs, cos_ref, sin_ref, peer_o, peer_qkv, relay, partials, landed, across_sent, across_landed,
    send_sems, recv_sems, load_sems, o_sems, qkv_sems, relay_send, relay_recv,
    direct_send, direct_recv, sum_send, sum_recv, across_sems, detour, detour_sems,
):
    me = lax.axis_index("tp")
    x, z = me % X_CHIPS, me // X_CHIPS
    right = z * X_CHIPS + (x + 1) % X_CHIPS
    left = z * X_CHIPS + (x + 3) % X_CHIPS
    far = z * X_CHIPS + (x + 2) % X_CHIPS
    across = (1 - z) * X_CHIPS + x
    across_right = (1 - z) * X_CHIPS + (x + 1) % X_CHIPS
    across_left = (1 - z) * X_CHIPS + (x + 3) % X_CHIPS
    across_far = (1 - z) * X_CHIPS + (x + 2) % X_CHIPS

    mine = lax.axis_index("rep")
    replicas = 2 * 2 * Y_CHIPS
    core, y, z_lo = mine % 2, mine // 2 % Y_CHIPS, mine // (2 * Y_CHIPS)
    target, origin = (mine + distance) % replicas, (mine + replicas - distance) % replicas
    around = distance <= 2
    back, ahead = (y + 3) % Y_CHIPS, (y + 1) % Y_CHIPS
    at_two, at_one = y // 2 * (1 - y % 2), (1 - y // 2) * (y % 2)
    hops_to = [
        replica(z_lo, back, core),
        replica((z_lo + at_two) % 2, back, core),
        replica(z_lo, back, core),
    ]
    hops_from = [
        replica(z_lo, ahead, core),
        replica((z_lo + at_one) % 2, ahead, core),
        replica(z_lo, ahead, core),
    ]
    if distance == 1:
        hops_to[2] = replica(z_lo, (y + 3 * core) % Y_CHIPS, 1 - core)
        hops_from[2] = replica(z_lo, (y + 1 - core) % Y_CHIPS, 1 - core)

    detours = DETOURS[distance]
    wraps = y + distance // 2 >= Y_CHIPS
    beside = replica(1 - z_lo, y, core)
    ahead_to = replica(z_lo, (y + distance // 2) % Y_CHIPS, core)
    ahead_from = replica(z_lo, (y + Y_CHIPS - distance // 2) % Y_CHIPS, core)

    if distance == 1:
        wraps = jnp.logical_and(y == Y_CHIPS - 1, core == 1)
        ahead_to = replica(z_lo, (y + core) % Y_CHIPS, 1 - core)
        ahead_from = replica(z_lo, (y + 3 * (1 - core)) % Y_CHIPS, 1 - core)

    barrier = pltpu.get_barrier_semaphore()
    for peer in (left, right, far, across):
        pl.semaphore_signal(barrier, inc=1, device_id={"tp": peer}, device_id_type=MESH)
    senders = [origin] + (hops_from if around else []) + ([beside, ahead_from] if detours else [])
    for peer in senders:
        pl.semaphore_signal(barrier, inc=1, device_id={"rep": peer}, device_id_type=MESH)
    loads = [
        pltpu.make_async_copy(src, dst, load_sems.at[index])
        for index, (src, dst) in enumerate(
            (
                (cot_in, cot),
                (wo_in, w_o),
                (x_in, x_all.at[me]),
                (wq_in, w_qkv.at[:, pl.ds(0, Q_COLS)]),
                (wk_in, w_qkv.at[:, pl.ds(Q_COLS, HEAD)]),
                (wv_in, w_qkv.at[:, pl.ds(Q_COLS + HEAD, HEAD)]),
                (docs_in, docs),
                (cos_in, cos_ref),
                (sin_in, sin_ref),
            )
        )
    ]
    for load in loads[:2]:
        load.start()
    pl.semaphore_wait(barrier, 4 + len(senders))

    def remote(src, dst, peer, index):
        return pltpu.make_async_remote_copy(
            src_ref=src, dst_ref=dst, send_sem=send_sems.at[index], recv_sem=recv_sems.at[index],
            device_id={"tp": peer}, device_id_type=MESH,
        )

    upper, lower = pl.ds(0, TOKENS // 2), pl.ds(TOKENS // 2, TOKENS // 2)
    own = x_all.at[me]
    to_right = remote(x_in, own, right, 0)
    to_left = remote(x_in, own, left, 1)
    to_across = remote(x_in, own, across, 2)
    part = x_all.at[left, upper]
    far_right = remote(part, part, right, 3)
    part = x_all.at[right, lower]
    far_left = remote(part, part, left, 4)
    part = x_all.at[across]
    across_to_right = remote(part, part, right, 5)
    across_to_left = remote(part, part, left, 6)
    part = x_all.at[far]
    far_to_across = remote(part, part, across, 7)

    to_right.start()
    to_left.start()
    to_across.start()
    for load in loads[2:]:
        load.start()
    for load in loads[:2]:
        load.wait()

    acc[:, :Q_COLS] = jnp.zeros((TOKENS, Q_COLS), F32)

    @pl.loop(0, TP)
    def _(step):
        columns = pl.ds(pl.multiple_of(step * SLAB, SLAB), SLAB)
        acc[:, :Q_COLS] += dot(cot[:, columns], w_o[:, columns], (1, 1))

    d_mixed[...] = (acc[:, :Q_COLS] * SCALE).astype(BF16)

    for load in loads[2:]:
        load.wait()

    acc[...] = jnp.zeros((TOKENS, QKV), F32)
    order = (me, left, right, across, far, across_left, across_right, across_far)

    def on_step_1():
        to_right.wait_recv()
        far_right.start()
        to_left.wait_recv()
        far_left.start()

    def on_step_2():
        to_across.wait_recv()
        across_to_right.start()
        across_to_left.start()

    def on_step_3():
        far_right.wait_recv()
        far_left.wait_recv()
        far_to_across.start()

    arrivals = {
        1: on_step_1,
        2: on_step_2,
        3: on_step_3,
        5: across_to_right.wait_recv,
        6: across_to_left.wait_recv,
        7: far_to_across.wait_recv,
    }

    @pl.loop(0, TP)
    def _(turn):
        block = order[0]
        for index in range(1, TP):
            block = jnp.where(turn == index, order[index], block)
        for index, arrival in arrivals.items():
            pl.when(turn == index)(arrival)
        rows = pl.ds(pl.multiple_of(block * SLAB, SLAB), SLAB)

        @pl.loop(0, QKV // 256)
        def _(step):
            columns = pl.ds(pl.multiple_of(step * 256, 256), 256)
            acc[:, columns] += dot(x_all[block], w_qkv[rows, columns], (1, 0))

        x_turned[rows, :] = x_all[block].T

    cosine, sine = cos_ref[...], sin_ref[...]
    later = lax.broadcasted_iota(jnp.int32, (SEQ, SEQ), 0)
    earlier = lax.broadcasted_iota(jnp.int32, (SEQ, SEQ), 1)
    causal = earlier <= later
    heads = range(Q_HEADS)

    @pl.loop(0, SEQS)
    def _(sequence):
        rows = pl.ds(pl.multiple_of(sequence * SEQ, SEQ), SEQ)

        def stacked(pieces):
            return jnp.concatenate(pieces, axis=0)

        queries = stacked(
            [
                turned(acc[rows, h * HEAD : (h + 1) * HEAD] * SCALE, cosine, sine).astype(BF16)
                for h in heads
            ]
        )
        keys = turned(acc[rows, Q_COLS : Q_COLS + HEAD] * SCALE, cosine, sine).astype(BF16)
        values = (acc[rows, Q_COLS + HEAD :] * SCALE).astype(BF16)
        number = jnp.broadcast_to(docs[pl.ds(sequence, 1), :].astype(F32), (SEQ, SEQ))
        allowed = jnp.logical_and(causal, number == number.T)
        scores = dot(queries, keys, (1, 1)) * SCORE_SCALE
        scores = stacked(
            [jnp.where(allowed, scores[h * SEQ : (h + 1) * SEQ], -1e9) for h in heads]
        )
        exps = jnp.exp(scores - jnp.max(scores, axis=1, keepdims=True))
        probs = exps / jnp.sum(exps, axis=1, keepdims=True)
        rounded = probs.astype(BF16)
        mixed = dot(rounded, values, (1, 0)).astype(BF16)
        d_heads = stacked([d_mixed[rows, h * HEAD : (h + 1) * HEAD] for h in heads])
        d_probs = dot(d_heads, values, (1, 1)).astype(BF16).astype(F32)
        d_values = dot(rounded, d_heads, (0, 0)).astype(BF16)
        d_scores = probs * (d_probs - jnp.sum(d_probs * probs, axis=1, keepdims=True))
        d_scores = (d_scores * SCORE_SCALE).astype(BF16)
        d_queries = dot(d_scores, keys, (1, 0)).astype(BF16).astype(F32)
        d_keys = dot(d_scores, queries, (0, 0)).astype(BF16).astype(F32)
        for h in heads:
            columns = slice(h * HEAD, (h + 1) * HEAD)
            stack = slice(h * SEQ, (h + 1) * SEQ)
            mixed_all[rows, columns] = mixed[stack]
            mixed_turned[columns, rows] = mixed[stack].T
            dqkv[rows, columns] = (turned(d_queries[stack], cosine, -sine) * SCALE).astype(BF16)
        dqkv[rows, Q_COLS : Q_COLS + HEAD] = (turned(d_keys, cosine, -sine) * SCALE).astype(BF16)
        dqkv[rows, Q_COLS + HEAD :] = (d_values.astype(F32) * SCALE).astype(BF16)

    rate = rate_ref[0]
    top, bottom = pl.ds(0, DIRECT_ROWS), pl.ds(DIRECT_ROWS, AROUND_ROWS)
    direct_rows = top if around else pl.ds(0, Q_COLS)

    def o_columns(step):
        return pl.ds(pl.multiple_of(step * O_COLS, O_COLS), O_COLS)

    def qkv_rows(step):
        return pl.ds(pl.multiple_of(step * SLAB, SLAB), SLAB)

    def sent_to(src, dst, sems, index, peer):
        return pltpu.make_async_remote_copy(
            src_ref=src, dst_ref=dst, send_sem=sems[0].at[index], recv_sem=sems[1].at[index],
            device_id={"rep": peer}, device_id_type=MESH,
        )

    def direct_o(step):
        part = (direct_rows, o_columns(step))
        return sent_to(u_o.at[part], peer_o.at[part], (direct_send, direct_recv), step, target)

    def direct_qkv(step):
        rows = qkv_rows(step)
        return sent_to(
            w_qkv.at[rows, :], peer_qkv.at[rows, :],
            (direct_send, direct_recv), O_STEPS + step, target,
        )

    def detoured(step):
        sems = (detour_sems.at[0], detour_sems.at[1])
        return sent_to(w_qkv.at[qkv_rows(step), :], detour.at[step], sems, step, beside)

    def handed_on(step):
        return sent_to(
            detour.at[step], peer_qkv.at[qkv_rows(step), :],
            (direct_send, direct_recv), O_STEPS + step, ahead_to,
        )

    def start_qkv(step):
        if step < detours:
            pl.when(wraps)(detoured(step).start)
            pl.when(jnp.logical_not(wraps))(direct_qkv(step).start)
        else:
            direct_qkv(step).start()

    def hand_on(*steps):
        def action():
            for step in steps:
                detoured(step).wait_recv()
                handed_on(step).start()

        pl.when(wraps)(action)

    def relayed(hop, step, own=False):
        columns = o_columns(step)
        src = u_o.at[bottom, columns] if own or hop == 0 else relay.at[hop - 1, :, columns]
        dst = peer_o.at[bottom, columns] if hop == 2 else relay.at[hop, :, columns]
        return sent_to(src, dst, (relay_send, relay_recv), hop * O_STEPS + step, hops_to[hop])

    def relaying(action):
        if distance == 1:
            pl.when(core == 1)(action)
        else:
            action()

    @pl.loop(0, O_STEPS)
    def _(step):
        columns = o_columns(step)

        @pl.loop(0, O_COLS // SLAB)
        def _(half):
            piece = pl.ds(pl.multiple_of(step * O_COLS + half * SLAB, SLAB), SLAB)
            gradient = dot(mixed_turned[...], cot[:, piece], (1, 0)) * SCALE
            u_o[:, piece] = moved(w_o[:, piece], gradient, rate)
        if around:
            relaying(lambda: relayed(0, step).start())
        if distance == 1:
            pl.when(core == 0)(lambda: relayed(2, step, own=True).start())
        direct_o(step).start()

    @pl.loop(0, TP)
    def _(step):
        rows = qkv_rows(step)
        gradient = dot(x_turned[rows, :], dqkv[...], (1, 0))
        w_qkv[rows, :] = moved(w_qkv[rows, :], gradient, rate)

    for step in range(detours + WINDOW - O_STEPS):
        start_qkv(step)

    def partial(to_x, to_z, half):
        owner = to_z * X_CHIPS + to_x
        columns = pl.ds(pl.multiple_of(owner * SLAB + half * 256, 256), 256)
        return dot(mixed_all[...], w_o[:, columns], (1, 0)) * SCALE

    def half_slab(half):
        return pl.ds(pl.multiple_of(half * 256, 256), 256)

    def sum_copy(slot):
        to_x = (x + slot % 3 + 1) % X_CHIPS
        return pltpu.make_async_remote_copy(
            src_ref=partials.at[slot], dst_ref=landed.at[slot],
            send_sem=sum_send.at[slot], recv_sem=sum_recv.at[slot],
            device_id={"tp": z * X_CHIPS + to_x}, device_id_type=MESH,
        )

    @pl.loop(0, 6)
    def _(slot):
        to_x = (x + slot % 3 + 1) % X_CHIPS
        to_z = (z + 1 + slot // 3) % 2

        @pl.loop(0, 2)
        def _(half):
            partials[slot, :, half_slab(half)] = partial(to_x, to_z, half).astype(BF16)

        sum_copy(slot).start()

    def summed(plane, to_z, into, extra=None):
        for slot in range(plane * 3, plane * 3 + 3):
            sum_copy(slot).wait_recv()

        @pl.loop(0, 2)
        def _(half):
            columns = half_slab(half)
            total = partial(x, to_z, half)
            for slot in range(plane * 3, plane * 3 + 3):
                total += landed[slot, :, columns].astype(F32)
            if extra is not None:
                total += extra[:, columns].astype(F32)
            into[:, columns] = total.astype(BF16)

    def crossing(part):
        rows = pl.ds(part * CROSSING_ROWS, CROSSING_ROWS)
        return pltpu.make_async_remote_copy(
            src_ref=across_sent.at[rows, :], dst_ref=across_landed.at[rows, :],
            send_sem=across_sems.at[0, part], recv_sem=across_sems.at[1, part],
            device_id={"tp": across}, device_id_type=MESH,
        )

    crossings = [crossing(part) for part in range(CROSSINGS)]

    def cross():
        summed(0, 1 - z, across_sent)
        for copy in crossings:
            copy.start()

    def finish_output():
        for copy in crossings:
            copy.wait_recv()
        summed(1, z, layer_out, across_landed)

    def averaged(own, peer, first_row, rows, columns):
        @pl.loop(0, rows // 16)
        def _(step):
            part = pl.ds(pl.multiple_of(first_row + step * 16, 16), 16)
            total = own[part, columns].astype(F32) + peer[part, columns].astype(F32)
            peer[part, columns] = (0.5 * total).astype(BF16)

    def store_o(step, index, rows):
        part = (rows, o_columns(step))
        return pltpu.make_async_copy(peer_o.at[part], o_out.at[part], o_sems.at[step, index])

    def store_qkv(step):
        rows = qkv_rows(step)
        return pltpu.make_async_copy(peer_qkv.at[rows, :], qkv_out.at[rows, :], qkv_sems.at[step])

    def arrived(index):
        if index + detours + WINDOW < O_STEPS + TP:
            start_qkv(index + detours + WINDOW - O_STEPS)
        if index < O_STEPS:
            direct_o(index).wait_recv()
            averaged(u_o, peer_o, 0, DIRECT_ROWS if around else Q_COLS, o_columns(index))
            store_o(index, 0, direct_rows).start()
        else:
            step = (index - O_STEPS + detours) % TP
            direct_qkv(step).wait_recv()
            averaged(w_qkv, peer_qkv, step * SLAB, SLAB, slice(None))
            store_qkv(step).start()

    def pass_on(hop):
        def action():
            @pl.loop(0, O_STEPS)
            def _(step):
                relayed(hop - 1, step).wait_recv()
                relayed(hop, step).start()

        relaying(action)

    events = {
        1: {
            2: [lambda: hand_on(0)],
            3: [lambda: pass_on(1)],
            5: [lambda: pass_on(2)],
            6: [cross],
        },
        2: {
            1: [lambda: hand_on(0)],
            3: [lambda: pass_on(1)],
            4: [cross],
            5: [lambda: pass_on(2)],
        },
        4: {1: [lambda: hand_on(0), cross], 2: [lambda: hand_on(1, 2)]},
        8: {1: [cross]},
    }[distance]
    for index in range(O_STEPS + TP):
        arrived(index)
        for event in events.get(index, ()):
            event()

    finish_output()
    if around:
        for step in range(O_STEPS):
            relayed(2, step).wait_recv()
            averaged(u_o, peer_o, DIRECT_ROWS, AROUND_ROWS, o_columns(step))
            store_o(step, 1, bottom).start()

    for step in range(O_STEPS):
        direct_o(step).wait_send()
        store_o(step, 0, direct_rows).wait()
        if around:
            store_o(step, 1, bottom).wait()
            relayed(2, step).wait_send()
    for step in range(TP):
        direct_qkv(step).wait_send()
        store_qkv(step).wait()
    for step in range(detours):
        pl.when(wraps)(detoured(step).wait_send)
    if around:

        def relays_sent():
            for step in range(O_STEPS):
                relayed(0, step).wait_send()
                relayed(1, step).wait_send()

        relaying(relays_sent)
    for copy in (
        to_right, to_left, to_across, far_right, far_left,
        across_to_right, across_to_left, far_to_across, *map(sum_copy, range(6)), *crossings,
    ):
        copy.wait_send()


def step(distance, normed, cotangent, w_query, w_key, w_value, w_out, documents, rate):
    cosine, sine = rotation_tables()
    hbm = pl.BlockSpec(memory_space=pl.ANY)
    vmem = pl.BlockSpec(memory_space=pltpu.VMEM)
    dma = pltpu.SemaphoreType.DMA
    block = (TOKENS, SLAB)
    layer_out, new_qkv, new_o = pl.pallas_call(
        functools.partial(step_kernel, distance),
        name="step_%d" % distance,
        out_shape=(
            jax.ShapeDtypeStruct(block, BF16),
            jax.ShapeDtypeStruct((D, QKV), BF16),
            jax.ShapeDtypeStruct((Q_COLS, D), BF16),
        ),
        in_specs=[hbm] * 9 + [pl.BlockSpec(memory_space=pltpu.SMEM)],
        out_specs=(vmem, hbm, hbm),
        scratch_shapes=[
            pltpu.VMEM((TP, TOKENS, SLAB), BF16),
            pltpu.VMEM((D, TOKENS), BF16),
            pltpu.VMEM((TOKENS, D), BF16),
            pltpu.VMEM((D, QKV), BF16),
            pltpu.VMEM((Q_COLS, D), BF16),
            pltpu.VMEM((Q_COLS, D), BF16),
            pltpu.VMEM((TOKENS, QKV), F32),
            pltpu.VMEM((TOKENS, Q_COLS), BF16),
            pltpu.VMEM((TOKENS, QKV), BF16),
            pltpu.VMEM((TOKENS, Q_COLS), BF16),
            pltpu.VMEM((Q_COLS, TOKENS), BF16),
            pltpu.VMEM((SEQS, SEQ), jnp.int32),
            pltpu.VMEM((SEQ, HEAD), F32),
            pltpu.VMEM((SEQ, HEAD), F32),
            pltpu.VMEM((Q_COLS, D), BF16),
            pltpu.VMEM((D, QKV), BF16),
            pltpu.VMEM((2, AROUND_ROWS, D), BF16) if distance <= 2 else pltpu.VMEM((2, 16, 128), BF16),
            pltpu.VMEM((6, *block), BF16),
            pltpu.VMEM((6, *block), BF16),
            pltpu.VMEM(block, BF16),
            pltpu.VMEM(block, BF16),
            dma((8,)),
            dma((8,)),
            dma((9,)),
            dma((O_STEPS, 2)),
            dma((TP,)),
            dma((3 * O_STEPS,)),
            dma((3 * O_STEPS,)),
            dma((O_STEPS + TP,)),
            dma((O_STEPS + TP,)),
            dma((6,)),
            dma((6,)),
            dma((2, CROSSINGS)),
            pltpu.VMEM((DETOURS[distance], SLAB, QKV) if DETOURS[distance] else (1, 16, 128), BF16),
            dma((2, max(1, DETOURS[distance]))),
        ],
        compiler_params=pltpu.CompilerParams(
            collective_id=distance, has_side_effects=True, vmem_limit_bytes=62 * 1024 * 1024
        ),
        cost_estimate=pl.CostEstimate(
            flops=14_000_000_000, bytes_accessed=30_000_000, transcendentals=300_000
        ),
    )(normed, cotangent, w_query, w_key, w_value, w_out, documents, cosine, sine, rate)
    new = (
        new_qkv[:, :Q_COLS], new_qkv[:, Q_COLS : Q_COLS + HEAD], new_qkv[:, Q_COLS + HEAD :], new_o
    )
    return (layer_out.reshape(SEQS, SEQ, SLAB), *(n[None] for n in new))


def per_device(normed, documents, cotangent, w_query, w_key, w_value, w_out, step_index):
    levels = lax.axis_size("rep").bit_length() - 1
    level = step_index[0] % levels
    rate = 3.0 * 32.0 / (32.0 + step_index.astype(F32))
    return lax.switch(
        level,
        [functools.partial(step, 2**exponent) for exponent in range(levels)],
        normed.reshape(TOKENS, SLAB), cotangent.reshape(TOKENS, D),
        w_query[0], w_key[0], w_value[0], w_out[0], documents, rate,
    )


def solution(mesh):
    in_specs = (
        P("rep", None, "tp"),
        P("rep", None),
        P("rep", None, None),
        P("rep", None, "tp"),
        P("rep", None, "tp"),
        P("rep", None, "tp"),
        P("rep", "tp", None),
        P(),
    )
    out_specs = (
        P("rep", None, "tp"),
        P("rep", None, "tp"),
        P("rep", None, "tp"),
        P("rep", None, "tp"),
        P("rep", "tp", None),
    )
    return jax.shard_map(
        per_device, mesh=mesh, in_specs=in_specs, out_specs=out_specs, check_vma=False
    )
```

```python
import functools
import math

import jax
import jax.numpy as jnp
import numpy as np
from jax import lax
from jax.experimental import pallas as pl
from jax.experimental.pallas import tpu as pltpu
from jax.sharding import PartitionSpec as P

HEAD = 128
SEQS = 4
SEQ = 128
TOKENS = SEQS * SEQ
X_CHIPS = 4
Y_CHIPS = 4
TP = 8
D = 4096
SLAB = D // TP
Q_HEADS = 4
Q_COLS = Q_HEADS * HEAD
QKV = Q_COLS + 2 * HEAD
DIRECT_ROWS = 192
AROUND_ROWS = Q_COLS - DIRECT_ROWS
O_STEPS = 4
O_COLS = D // O_STEPS
WINDOW = 6
CROSSINGS = 8
CROSSING_ROWS = TOKENS // CROSSINGS
DETOURS = {1: 1, 2: 1, 4: 3, 8: 0}
SCALE = 1.0 / math.sqrt(D)
SCORE_SCALE = 1.0 / math.sqrt(HEAD)
MESH = pl.DeviceIdType.MESH
F32 = jnp.float32
BF16 = jnp.bfloat16


def rotation_tables():
    half = HEAD // 2
    frequency = (500000.0 ** (-np.arange(half, dtype=np.float64) / half)).astype(np.float32)
    angles = np.arange(SEQ, dtype=np.float32)[:, None] * frequency[None, :]
    cosine, sine = np.cos(angles), np.sin(angles)
    return (
        np.concatenate([cosine, cosine], axis=1).astype(np.float32),
        np.concatenate([-sine, sine], axis=1).astype(np.float32),
    )


def dot(a, b, contract):
    return lax.dot_general(
        a, b, (((contract[0],), (contract[1],)), ((), ())), preferred_element_type=F32
    )


def turned(values, cosine, sine):
    return values * cosine + pltpu.roll(values, HEAD // 2, 1) * sine


def moved(weight, gradient, rate):
    gradient = gradient.astype(BF16).astype(F32)
    return (weight.astype(F32) - rate * gradient).astype(BF16)


def replica(z, y, core):
    return (z * Y_CHIPS + y) * 2 + core


def step_kernel(
    distance,
    x_in, cot_in, wq_in, wk_in, wv_in, wo_in, docs_in, cos_in, sin_in, rate_ref,
    layer_out, qkv_out, o_out,
    x_all, x_turned, cot, w_qkv, w_o, u_o, acc, d_mixed, dqkv, mixed_all, mixed_turned,
    docs, cos_ref, sin_ref, peer_o, peer_qkv, relay, partials, landed, across_sent, across_landed,
    send_sems, recv_sems, load_sems, o_sems, qkv_sems, relay_send, relay_recv,
    direct_send, direct_recv, sum_send, sum_recv, across_sems, detour, detour_sems,
):
    me = lax.axis_index("tp")
    x, z = me % X_CHIPS, me // X_CHIPS
    right = z * X_CHIPS + (x + 1) % X_CHIPS
    left = z * X_CHIPS + (x + 3) % X_CHIPS
    far = z * X_CHIPS + (x + 2) % X_CHIPS
    across = (1 - z) * X_CHIPS + x
    across_right = (1 - z) * X_CHIPS + (x + 1) % X_CHIPS
    across_left = (1 - z) * X_CHIPS + (x + 3) % X_CHIPS
    across_far = (1 - z) * X_CHIPS + (x + 2) % X_CHIPS

    mine = lax.axis_index("rep")
    replicas = 2 * 2 * Y_CHIPS
    core, y, z_lo = mine % 2, mine // 2 % Y_CHIPS, mine // (2 * Y_CHIPS)
    target, origin = (mine + distance) % replicas, (mine + replicas - distance) % replicas
    around = distance <= 2
    back, ahead = (y + 3) % Y_CHIPS, (y + 1) % Y_CHIPS
    at_two, at_one = y // 2 * (1 - y % 2), (1 - y // 2) * (y % 2)
    hops_to = [
        replica(z_lo, back, core),
        replica((z_lo + at_two) % 2, back, core),
        replica(z_lo, back, core),
    ]
    hops_from = [
        replica(z_lo, ahead, core),
        replica((z_lo + at_one) % 2, ahead, core),
        replica(z_lo, ahead, core),
    ]
    if distance == 1:
        hops_to[2] = replica(z_lo, (y + 3 * core) % Y_CHIPS, 1 - core)
        hops_from[2] = replica(z_lo, (y + 1 - core) % Y_CHIPS, 1 - core)

    detours = DETOURS[distance]
    wraps = y + distance // 2 >= Y_CHIPS
    beside = replica(1 - z_lo, y, core)
    ahead_to = replica(z_lo, (y + distance // 2) % Y_CHIPS, core)
    ahead_from = replica(z_lo, (y + Y_CHIPS - distance // 2) % Y_CHIPS, core)

    if distance == 1:
        wraps = jnp.logical_and(y == Y_CHIPS - 1, core == 1)
        ahead_to = replica(z_lo, (y + core) % Y_CHIPS, 1 - core)
        ahead_from = replica(z_lo, (y + 3 * (1 - core)) % Y_CHIPS, 1 - core)

    barrier = pltpu.get_barrier_semaphore()
    for peer in (left, right, far, across):
        pl.semaphore_signal(barrier, inc=1, device_id={"tp": peer}, device_id_type=MESH)
    senders = [origin] + (hops_from if around else []) + ([beside, ahead_from] if detours else [])
    for peer in senders:
        pl.semaphore_signal(barrier, inc=1, device_id={"rep": peer}, device_id_type=MESH)
    loads = [
        pltpu.make_async_copy(src, dst, load_sems.at[index])
        for index, (src, dst) in enumerate(
            (
                (cot_in, cot),
                (wo_in, w_o),
                (x_in, x_all.at[me]),
                (wq_in, w_qkv.at[:, pl.ds(0, Q_COLS)]),
                (wk_in, w_qkv.at[:, pl.ds(Q_COLS, HEAD)]),
                (wv_in, w_qkv.at[:, pl.ds(Q_COLS + HEAD, HEAD)]),
                (docs_in, docs),
                (cos_in, cos_ref),
                (sin_in, sin_ref),
            )
        )
    ]
    for load in loads[:2]:
        load.start()
    pl.semaphore_wait(barrier, 4 + len(senders))

    def remote(src, dst, peer, index):
        return pltpu.make_async_remote_copy(
            src_ref=src, dst_ref=dst, send_sem=send_sems.at[index], recv_sem=recv_sems.at[index],
            device_id={"tp": peer}, device_id_type=MESH,
        )

    upper, lower = pl.ds(0, TOKENS // 2), pl.ds(TOKENS // 2, TOKENS // 2)
    own = x_all.at[me]
    to_right = remote(x_in, own, right, 0)
    to_left = remote(x_in, own, left, 1)
    to_across = remote(x_in, own, across, 2)
    part = x_all.at[left, upper]
    far_right = remote(part, part, right, 3)
    part = x_all.at[right, lower]
    far_left = remote(part, part, left, 4)
    part = x_all.at[across]
    across_to_right = remote(part, part, right, 5)
    across_to_left = remote(part, part, left, 6)
    part = x_all.at[far]
    far_to_across = remote(part, part, across, 7)

    to_right.start()
    to_left.start()
    to_across.start()
    for load in loads[2:]:
        load.start()
    for load in loads[:2]:
        load.wait()

    acc[:, :Q_COLS] = jnp.zeros((TOKENS, Q_COLS), F32)

    @pl.loop(0, TP)
    def _(step):
        columns = pl.ds(pl.multiple_of(step * SLAB, SLAB), SLAB)
        acc[:, :Q_COLS] += dot(cot[:, columns], w_o[:, columns], (1, 1))

    d_mixed[...] = (acc[:, :Q_COLS] * SCALE).astype(BF16)

    for load in loads[2:]:
        load.wait()

    acc[...] = jnp.zeros((TOKENS, QKV), F32)
    order = (me, left, right, across, far, across_left, across_right, across_far)

    def on_step_1():
        to_right.wait_recv()
        far_right.start()
        to_left.wait_recv()
        far_left.start()

    def on_step_2():
        to_across.wait_recv()
        across_to_right.start()
        across_to_left.start()

    def on_step_3():
        far_right.wait_recv()
        far_left.wait_recv()
        far_to_across.start()

    arrivals = {
        1: on_step_1,
        2: on_step_2,
        3: on_step_3,
        5: across_to_right.wait_recv,
        6: across_to_left.wait_recv,
        7: far_to_across.wait_recv,
    }

    @pl.loop(0, TP)
    def _(turn):
        block = order[0]
        for index in range(1, TP):
            block = jnp.where(turn == index, order[index], block)
        for index, arrival in arrivals.items():
            pl.when(turn == index)(arrival)
        rows = pl.ds(pl.multiple_of(block * SLAB, SLAB), SLAB)

        @pl.loop(0, QKV // 256)
        def _(step):
            columns = pl.ds(pl.multiple_of(step * 256, 256), 256)
            acc[:, columns] += dot(x_all[block], w_qkv[rows, columns], (1, 0))

        x_turned[rows, :] = x_all[block].T

    cosine, sine = cos_ref[...], sin_ref[...]
    later = lax.broadcasted_iota(jnp.int32, (SEQ, SEQ), 0)
    earlier = lax.broadcasted_iota(jnp.int32, (SEQ, SEQ), 1)
    causal = earlier <= later
    heads = range(Q_HEADS)

    @pl.loop(0, SEQS)
    def _(sequence):
        rows = pl.ds(pl.multiple_of(sequence * SEQ, SEQ), SEQ)

        def stacked(pieces):
            return jnp.concatenate(pieces, axis=0)

        queries = stacked(
            [
                turned(acc[rows, h * HEAD : (h + 1) * HEAD] * SCALE, cosine, sine).astype(BF16)
                for h in heads
            ]
        )
        keys = turned(acc[rows, Q_COLS : Q_COLS + HEAD] * SCALE, cosine, sine).astype(BF16)
        values = (acc[rows, Q_COLS + HEAD :] * SCALE).astype(BF16)
        number = jnp.broadcast_to(docs[pl.ds(sequence, 1), :].astype(F32), (SEQ, SEQ))
        allowed = jnp.logical_and(causal, number == number.T)
        scores = dot(queries, keys, (1, 1)) * SCORE_SCALE
        scores = stacked(
            [jnp.where(allowed, scores[h * SEQ : (h + 1) * SEQ], -1e9) for h in heads]
        )
        exps = jnp.exp(scores - jnp.max(scores, axis=1, keepdims=True))
        probs = exps / jnp.sum(exps, axis=1, keepdims=True)
        rounded = probs.astype(BF16)
        mixed = dot(rounded, values, (1, 0)).astype(BF16)
        d_heads = stacked([d_mixed[rows, h * HEAD : (h + 1) * HEAD] for h in heads])
        d_probs = dot(d_heads, values, (1, 1)).astype(BF16).astype(F32)
        d_values = dot(rounded, d_heads, (0, 0)).astype(BF16)
        d_scores = probs * (d_probs - jnp.sum(d_probs * probs, axis=1, keepdims=True))
        d_scores = (d_scores * SCORE_SCALE).astype(BF16)
        d_queries = dot(d_scores, keys, (1, 0)).astype(BF16).astype(F32)
        d_keys = dot(d_scores, queries, (0, 0)).astype(BF16).astype(F32)
        for h in heads:
            columns = slice(h * HEAD, (h + 1) * HEAD)
            stack = slice(h * SEQ, (h + 1) * SEQ)
            mixed_all[rows, columns] = mixed[stack]
            mixed_turned[columns, rows] = mixed[stack].T
            dqkv[rows, columns] = (turned(d_queries[stack], cosine, -sine) * SCALE).astype(BF16)
        dqkv[rows, Q_COLS : Q_COLS + HEAD] = (turned(d_keys, cosine, -sine) * SCALE).astype(BF16)
        dqkv[rows, Q_COLS + HEAD :] = (d_values.astype(F32) * SCALE).astype(BF16)

    rate = rate_ref[0]
    top, bottom = pl.ds(0, DIRECT_ROWS), pl.ds(DIRECT_ROWS, AROUND_ROWS)
    direct_rows = top if around else pl.ds(0, Q_COLS)

    def o_columns(step):
        return pl.ds(pl.multiple_of(step * O_COLS, O_COLS), O_COLS)

    def qkv_rows(step):
        return pl.ds(pl.multiple_of(step * SLAB, SLAB), SLAB)

    def sent_to(src, dst, sems, index, peer):
        return pltpu.make_async_remote_copy(
            src_ref=src, dst_ref=dst, send_sem=sems[0].at[index], recv_sem=sems[1].at[index],
            device_id={"rep": peer}, device_id_type=MESH,
        )

    def direct_o(step):
        part = (direct_rows, o_columns(step))
        return sent_to(u_o.at[part], peer_o.at[part], (direct_send, direct_recv), step, target)

    def direct_qkv(step):
        rows = qkv_rows(step)
        return sent_to(
            w_qkv.at[rows, :], peer_qkv.at[rows, :],
            (direct_send, direct_recv), O_STEPS + step, target,
        )

    def detoured(step):
        sems = (detour_sems.at[0], detour_sems.at[1])
        return sent_to(w_qkv.at[qkv_rows(step), :], detour.at[step], sems, step, beside)

    def handed_on(step):
        return sent_to(
            detour.at[step], peer_qkv.at[qkv_rows(step), :],
            (direct_send, direct_recv), O_STEPS + step, ahead_to,
        )

    def start_qkv(step):
        if step < detours:
            pl.when(wraps)(detoured(step).start)
            pl.when(jnp.logical_not(wraps))(direct_qkv(step).start)
        else:
            direct_qkv(step).start()

    def hand_on(*steps):
        def action():
            for step in steps:
                detoured(step).wait_recv()
                handed_on(step).start()

        pl.when(wraps)(action)

    def relayed(hop, step, own=False):
        columns = o_columns(step)
        src = u_o.at[bottom, columns] if own or hop == 0 else relay.at[hop - 1, :, columns]
        dst = peer_o.at[bottom, columns] if hop == 2 else relay.at[hop, :, columns]
        return sent_to(src, dst, (relay_send, relay_recv), hop * O_STEPS + step, hops_to[hop])

    def relaying(action):
        if distance == 1:
            pl.when(core == 1)(action)
        else:
            action()

    @pl.loop(0, O_STEPS)
    def _(step):
        columns = o_columns(step)

        @pl.loop(0, O_COLS // SLAB)
        def _(half):
            piece = pl.ds(pl.multiple_of(step * O_COLS + half * SLAB, SLAB), SLAB)
            gradient = dot(mixed_turned[...], cot[:, piece], (1, 0)) * SCALE
            u_o[:, piece] = moved(w_o[:, piece], gradient, rate)
        if around:
            relaying(lambda: relayed(0, step).start())
        if distance == 1:
            pl.when(core == 0)(lambda: relayed(2, step, own=True).start())
        direct_o(step).start()

    @pl.loop(0, TP)
    def _(step):
        rows = qkv_rows(step)
        gradient = dot(x_turned[rows, :], dqkv[...], (1, 0))
        w_qkv[rows, :] = moved(w_qkv[rows, :], gradient, rate)

    for step in range(detours + WINDOW - O_STEPS):
        start_qkv(step)

    def partial(to_x, to_z, half):
        owner = to_z * X_CHIPS + to_x
        columns = pl.ds(pl.multiple_of(owner * SLAB + half * 256, 256), 256)
        return dot(mixed_all[...], w_o[:, columns], (1, 0)) * SCALE

    def half_slab(half):
        return pl.ds(pl.multiple_of(half * 256, 256), 256)

    def sum_copy(slot):
        to_x = (x + slot % 3 + 1) % X_CHIPS
        return pltpu.make_async_remote_copy(
            src_ref=partials.at[slot], dst_ref=landed.at[slot],
            send_sem=sum_send.at[slot], recv_sem=sum_recv.at[slot],
            device_id={"tp": z * X_CHIPS + to_x}, device_id_type=MESH,
        )

    @pl.loop(0, 6)
    def _(slot):
        to_x = (x + slot % 3 + 1) % X_CHIPS
        to_z = (z + 1 + slot // 3) % 2

        @pl.loop(0, 2)
        def _(half):
            partials[slot, :, half_slab(half)] = partial(to_x, to_z, half).astype(BF16)

        sum_copy(slot).start()

    def summed(plane, to_z, into, extra=None):
        for slot in range(plane * 3, plane * 3 + 3):
            sum_copy(slot).wait_recv()

        @pl.loop(0, 2)
        def _(half):
            columns = half_slab(half)
            total = partial(x, to_z, half)
            for slot in range(plane * 3, plane * 3 + 3):
                total += landed[slot, :, columns].astype(F32)
            if extra is not None:
                total += extra[:, columns].astype(F32)
            into[:, columns] = total.astype(BF16)

    def crossing(part):
        rows = pl.ds(part * CROSSING_ROWS, CROSSING_ROWS)
        return pltpu.make_async_remote_copy(
            src_ref=across_sent.at[rows, :], dst_ref=across_landed.at[rows, :],
            send_sem=across_sems.at[0, part], recv_sem=across_sems.at[1, part],
            device_id={"tp": across}, device_id_type=MESH,
        )

    crossings = [crossing(part) for part in range(CROSSINGS)]

    def cross():
        summed(0, 1 - z, across_sent)
        for copy in crossings:
            copy.start()

    def finish_output():
        for copy in crossings:
            copy.wait_recv()
        summed(1, z, layer_out, across_landed)

    def averaged(own, peer, first_row, rows, columns):
        @pl.loop(0, rows // 16)
        def _(step):
            part = pl.ds(pl.multiple_of(first_row + step * 16, 16), 16)
            total = own[part, columns].astype(F32) + peer[part, columns].astype(F32)
            peer[part, columns] = (0.5 * total).astype(BF16)

    def store_o(step, index, rows):
        part = (rows, o_columns(step))
        return pltpu.make_async_copy(peer_o.at[part], o_out.at[part], o_sems.at[step, index])

    def store_qkv(step):
        rows = qkv_rows(step)
        return pltpu.make_async_copy(peer_qkv.at[rows, :], qkv_out.at[rows, :], qkv_sems.at[step])

    def arrived(index):
        if index + detours + WINDOW < O_STEPS + TP:
            start_qkv(index + detours + WINDOW - O_STEPS)
        if index < O_STEPS:
            direct_o(index).wait_recv()
            averaged(u_o, peer_o, 0, DIRECT_ROWS if around else Q_COLS, o_columns(index))
            store_o(index, 0, direct_rows).start()
        else:
            step = (index - O_STEPS + detours) % TP
            direct_qkv(step).wait_recv()
            averaged(w_qkv, peer_qkv, step * SLAB, SLAB, slice(None))
            store_qkv(step).start()

    def pass_on(hop):
        def action():
            @pl.loop(0, O_STEPS)
            def _(step):
                relayed(hop - 1, step).wait_recv()
                relayed(hop, step).start()

        relaying(action)

    events = {
        1: {
            2: [lambda: hand_on(0)],
            3: [lambda: pass_on(1)],
            5: [lambda: pass_on(2)],
            6: [cross],
        },
        2: {
            1: [lambda: hand_on(0)],
            3: [lambda: pass_on(1)],
            4: [cross],
            5: [lambda: pass_on(2)],
        },
        4: {1: [lambda: hand_on(0), cross], 2: [lambda: hand_on(1, 2)], 10: [finish_output]},
        8: {1: [cross], 10: [finish_output]},
    }[distance]
    for index in range(O_STEPS + TP):
        arrived(index)
        for event in events.get(index, ()):
            event()

    if around:
        finish_output()
        for step in range(O_STEPS):
            relayed(2, step).wait_recv()
            averaged(u_o, peer_o, DIRECT_ROWS, AROUND_ROWS, o_columns(step))
            store_o(step, 1, bottom).start()

    for step in range(O_STEPS):
        direct_o(step).wait_send()
        store_o(step, 0, direct_rows).wait()
        if around:
            store_o(step, 1, bottom).wait()
            relayed(2, step).wait_send()
    for step in range(TP):
        direct_qkv(step).wait_send()
        store_qkv(step).wait()
    for step in range(detours):
        pl.when(wraps)(detoured(step).wait_send)
    if around:

        def relays_sent():
            for step in range(O_STEPS):
                relayed(0, step).wait_send()
                relayed(1, step).wait_send()

        relaying(relays_sent)
    for copy in (
        to_right, to_left, to_across, far_right, far_left,
        across_to_right, across_to_left, far_to_across, *map(sum_copy, range(6)), *crossings,
    ):
        copy.wait_send()


def step(distance, normed, cotangent, w_query, w_key, w_value, w_out, documents, rate):
    cosine, sine = rotation_tables()
    hbm = pl.BlockSpec(memory_space=pl.ANY)
    vmem = pl.BlockSpec(memory_space=pltpu.VMEM)
    dma = pltpu.SemaphoreType.DMA
    block = (TOKENS, SLAB)
    layer_out, new_qkv, new_o = pl.pallas_call(
        functools.partial(step_kernel, distance),
        name="step_%d" % distance,
        out_shape=(
            jax.ShapeDtypeStruct(block, BF16),
            jax.ShapeDtypeStruct((D, QKV), BF16),
            jax.ShapeDtypeStruct((Q_COLS, D), BF16),
        ),
        in_specs=[hbm] * 9 + [pl.BlockSpec(memory_space=pltpu.SMEM)],
        out_specs=(vmem, hbm, hbm),
        scratch_shapes=[
            pltpu.VMEM((TP, TOKENS, SLAB), BF16),
            pltpu.VMEM((D, TOKENS), BF16),
            pltpu.VMEM((TOKENS, D), BF16),
            pltpu.VMEM((D, QKV), BF16),
            pltpu.VMEM((Q_COLS, D), BF16),
            pltpu.VMEM((Q_COLS, D), BF16),
            pltpu.VMEM((TOKENS, QKV), F32),
            pltpu.VMEM((TOKENS, Q_COLS), BF16),
            pltpu.VMEM((TOKENS, QKV), BF16),
            pltpu.VMEM((TOKENS, Q_COLS), BF16),
            pltpu.VMEM((Q_COLS, TOKENS), BF16),
            pltpu.VMEM((SEQS, SEQ), jnp.int32),
            pltpu.VMEM((SEQ, HEAD), F32),
            pltpu.VMEM((SEQ, HEAD), F32),
            pltpu.VMEM((Q_COLS, D), BF16),
            pltpu.VMEM((D, QKV), BF16),
            pltpu.VMEM((2, AROUND_ROWS, D), BF16) if distance <= 2 else pltpu.VMEM((2, 16, 128), BF16),
            pltpu.VMEM((6, *block), BF16),
            pltpu.VMEM((6, *block), BF16),
            pltpu.VMEM(block, BF16),
            pltpu.VMEM(block, BF16),
            dma((8,)),
            dma((8,)),
            dma((9,)),
            dma((O_STEPS, 2)),
            dma((TP,)),
            dma((3 * O_STEPS,)),
            dma((3 * O_STEPS,)),
            dma((O_STEPS + TP,)),
            dma((O_STEPS + TP,)),
            dma((6,)),
            dma((6,)),
            dma((2, CROSSINGS)),
            pltpu.VMEM((DETOURS[distance], SLAB, QKV) if DETOURS[distance] else (1, 16, 128), BF16),
            dma((2, max(1, DETOURS[distance]))),
        ],
        compiler_params=pltpu.CompilerParams(
            collective_id=distance, has_side_effects=True, vmem_limit_bytes=62 * 1024 * 1024
        ),
        cost_estimate=pl.CostEstimate(
            flops=14_000_000_000, bytes_accessed=30_000_000, transcendentals=300_000
        ),
    )(normed, cotangent, w_query, w_key, w_value, w_out, documents, cosine, sine, rate)
    new = (
        new_qkv[:, :Q_COLS], new_qkv[:, Q_COLS : Q_COLS + HEAD], new_qkv[:, Q_COLS + HEAD :], new_o
    )
    return (layer_out.reshape(SEQS, SEQ, SLAB), *(n[None] for n in new))


def per_device(normed, documents, cotangent, w_query, w_key, w_value, w_out, step_index):
    levels = lax.axis_size("rep").bit_length() - 1
    level = step_index[0] % levels
    rate = 3.0 * 32.0 / (32.0 + step_index.astype(F32))
    return lax.switch(
        level,
        [functools.partial(step, 2**exponent) for exponent in range(levels)],
        normed.reshape(TOKENS, SLAB), cotangent.reshape(TOKENS, D),
        w_query[0], w_key[0], w_value[0], w_out[0], documents, rate,
    )


def solution(mesh):
    in_specs = (
        P("rep", None, "tp"),
        P("rep", None),
        P("rep", None, None),
        P("rep", None, "tp"),
        P("rep", None, "tp"),
        P("rep", None, "tp"),
        P("rep", "tp", None),
        P(),
    )
    out_specs = (
        P("rep", None, "tp"),
        P("rep", None, "tp"),
        P("rep", None, "tp"),
        P("rep", None, "tp"),
        P("rep", "tp", None),
    )
    return jax.shard_map(
        per_device, mesh=mesh, in_specs=in_specs, out_specs=out_specs, check_vma=False
    )
```
